256 devices in a mesh: real: 4 (over x_lo, core), space: 64 (over y, z, x_hi).
Axes of the slice: x: 4 (x_hi: 2, x_lo: 2; x = x_hi * 2 + x_lo), y: 4, z: 8, core: 2. Of those that a mesh axis runs over, the one named last changes fastest.
Arguments:
- perm_class: int32 [64, 16, 16, 128], P('space'), may hold values from 0 to 7
- class_values: float32 [8], replicated, may hold values from 0.3 to 10
- well_cells: int32 [64], P('real'), parts along dimension 0, may hold values from 0 to 2097151
- well_rates: float32 [64], P('real'), parts along dimension 0, may hold values from 0.5 to 3
- guess: float32 [256, 16, 16, 128], P(('real', 'space')), parts along dimension 0, may hold values from -4 to 4
Outputs:
- pressure: float32 [256, 16, 16, 128], P(('real', 'space')), parts along dimension 0
- residual: float32 [256, 16, 16, 128], P(('real', 'space')), parts along dimension 0
The draws below stay inside these ranges and needn't reach their ends.
There are 4 independent parts, one for each index of `real`. The reference program is written for one: setup_inputs(seed, part) draws one part's arguments, and reference() takes and returns one part's arrays. A program takes and returns all parts, laid end to end along the dimension named above; an argument that names none is the same for every part. Nothing has to cross between parts.
All inputs are finite; a program needn't handle non-finite values.
Results may differ from the reference program's by a relative error of at most 0.00015.
Values sent between devices are 32-bit elements; how exact they have to be, the bound alone decides.
A program may use at most 128 MiB of HBM per device.

```python
import math
import jax
import jax.numpy as jnp

CX = 16
CY = 16
CZ = 128
NCLASS = 8
NWELLS = 16
LEVELS = 3
SWEEPS = 2
CSWEEPS = 6
BLOCKS = 64
SIDE = 4
ROTATE = 21
NX = 64
NY = 64
NZ = 512


def place_ends(entries, stream_key, low, high):
    extent = entries.shape
    spot = [jax.random.randint(jax.random.fold_in(stream_key, axis), (), 0, extent[axis]) for axis in range(len(extent))]
    entries = entries.at[tuple(spot)].set(low)
    longest = extent.index(max(extent))
    spot[longest] = (spot[longest] + 1) % extent[longest]
    return entries.at[tuple(spot)].set(high)


def steps_of(rng, shape, shards, least, largest):
    gain, own = 1.0, jax.random.fold_in(rng, 6)
    for position, blocks in shards:
        draws = jnp.exp(jax.random.uniform(jax.random.fold_in(own, position), (blocks,), jnp.float32, least / len(shards), largest / len(shards)))
        gain = gain * jnp.repeat(draws, shape[position] // blocks).reshape([-1 if axis == position else 1 for axis in range(len(shape))])
    return gain


def bell_draw(rng, extent, width, most, split=(), held_as=jnp.bfloat16):
    factor_of = steps_of(rng, extent, split, -0.22, 0.18) if split else 1.0
    drawn = jax.random.normal(rng, extent, jnp.float32) * width * factor_of
    return jnp.minimum(jnp.maximum(drawn, -most), most).astype(held_as)


def setup_inputs(seed: int = 0, part: int = 0) -> dict:
    keys = jax.random.split(jax.random.key(seed), 6)
    part_keys = jax.random.split(jax.random.fold_in(keys[5], part), 6)
    return {
        "perm_class": place_ends(jax.random.randint(keys[0], (BLOCKS, CX, CY, CZ), 0, NCLASS), jax.random.fold_in(keys[0], 1), 0, NCLASS - 1).astype(jnp.int32),
        "class_values": jnp.clip(jnp.exp(jax.random.uniform(keys[1], (NCLASS,), jnp.float32, math.log(0.3), math.log(10.0))), 0.3, 10.0),
        "well_cells": place_ends(jax.random.randint(part_keys[2], (NWELLS,), 0, NX * NY * NZ), jax.random.fold_in(part_keys[2], 1), 0, (NX * NY * NZ) - 1).astype(jnp.int32),
        "well_rates": jnp.clip(jax.random.uniform(part_keys[3], (NWELLS,), jnp.float32, 0.5, 3.0), 0.5, 3.0),
        "guess": bell_draw(part_keys[4], (BLOCKS, CX, CY, CZ), 0.3, 4.0, ((0, 64),), jnp.float32),
    }


OMEGA = 0.8


def to_blocks(grid_vals):
    arranged = grid_vals.reshape(SIDE, CX, SIDE, CY, SIDE, CZ).transpose(0, 2, 4, 1, 3, 5)
    return jnp.roll(arranged.reshape(BLOCKS, CX, CY, CZ), -ROTATE, axis=0)


def rolled_faces(values, per_side):
    plane_step = per_side * per_side
    return [jnp.concatenate([jnp.roll(values[:, -1:], plane_step, axis=0), values[:, :-1]], axis=1),
            jnp.concatenate([values[:, 1:], jnp.roll(values[:, :1], -plane_step, axis=0)], axis=1),
            jnp.concatenate([jnp.roll(values[:, :, -1:], per_side, axis=0), values[:, :, :-1]], axis=2),
            jnp.concatenate([values[:, :, 1:], jnp.roll(values[:, :, :1], -per_side, axis=0)], axis=2),
            jnp.concatenate([jnp.roll(values[:, :, :, -1:], 1, axis=0), values[:, :, :, :-1]], axis=3),
            jnp.concatenate([values[:, :, :, 1:], jnp.roll(values[:, :, :, :1], -1, axis=0)], axis=3)]


def coefficients(permeab, neighbors, scaling):
    face_coefs = [0.5 * (permeab + beside) for beside in neighbors]
    total_sum = face_coefs[0]
    for number in range(1, 6):
        total_sum = total_sum + face_coefs[number]
    return face_coefs, scaling * total_sum


def operate(values, neighbors, face_coefs, scaling):
    total_sum = face_coefs[0] * (values - neighbors[0])
    for number in range(1, 6):
        total_sum = total_sum + face_coefs[number] * (values - neighbors[number])
    return scaling * total_sum


def smooth(values, right_side, face_coefs, diagonal, scaling):
    return values + OMEGA * (right_side - operate(values, rolled_faces(values, SIDE), face_coefs, scaling)) / diagonal


def coarsen(values):
    count_b, size_x, size_y, size_z = values.shape
    return values.reshape(count_b, size_x // 2, 2, size_y // 2, 2, size_z // 2, 2).mean(axis=(2, 4, 6))


def refine(values):
    return jnp.repeat(jnp.repeat(jnp.repeat(values, 2, axis=1), 2, axis=2), 2, axis=3)


def reference(perm_class, class_values, well_cells, well_rates, guess):
    permeab = jnp.zeros(perm_class.shape, jnp.float32)
    for number in range(NCLASS):
        permeab = permeab + jnp.where(perm_class == number, class_values[number], 0.0)
    source = to_blocks(jnp.zeros((NX * NY * NZ,), jnp.float32).at[well_cells].add(well_rates).reshape(NX, NY, NZ))
    perms = [permeab]
    for level_no in range(LEVELS):
        perms.append(coarsen(perms[-1]))
    coefs = [coefficients(perms[level_no], rolled_faces(perms[level_no], SIDE), 0.25 ** level_no) for level_no in range(LEVELS + 1)]
    values = guess
    right_side = source
    stored = []
    rights = []
    for level_no in range(LEVELS):
        face_coefs, diagonal = coefs[level_no]
        scaling = 0.25 ** level_no
        if level_no == 0:
            count_sw = SWEEPS
        else:
            values = OMEGA * right_side / diagonal
            count_sw = SWEEPS - 1
        for sweep_no in range(count_sw):
            values = smooth(values, right_side, face_coefs, diagonal, scaling)
        leftover = right_side - operate(values, rolled_faces(values, SIDE), face_coefs, scaling)
        stored.append(values)
        rights.append(right_side)
        right_side = coarsen(leftover)
    face_coefs, diagonal = coefs[LEVELS]
    scaling = 0.25 ** LEVELS
    correction = OMEGA * right_side / diagonal
    for sweep_no in range(CSWEEPS - 1):
        correction = smooth(correction, right_side, face_coefs, diagonal, scaling)
    for level_no in reversed(range(LEVELS)):
        face_coefs, diagonal = coefs[level_no]
        scaling = 0.25 ** level_no
        values = stored[level_no] + refine(correction)
        for sweep_no in range(SWEEPS):
            values = smooth(values, rights[level_no], face_coefs, diagonal, scaling)
        correction = values
    residual = source - operate(correction, rolled_faces(correction, SIDE), coefs[0][0], 1.0)
    return correction, residual
```

```python
import functools

import jax
import jax.numpy as jnp
from jax import lax
from jax.experimental import pallas as pl
from jax.experimental.pallas import tpu as pltpu
from jax.sharding import PartitionSpec as P

N = 64
ROTATE = 21
OMEGA = 0.8
F32 = jnp.float32
HI = lax.Precision.HIGHEST
DIRS = [(a, b, c) for a in (-1, 0, 1) for b in (-1, 0, 1) for c in (-1, 0, 1) if (a, b, c) != (0, 0, 0)]


def offset(d):
    return (16 * d[0] + 4 * d[1] + d[2]) % N


def plan0(narr):
    x_at = {1: 0, -1: 6 * narr}
    y_at = {1: 12 * narr, -1: 20 * narr}
    z_at = {1: 28 * narr, -1: 28 * narr + 2}
    plan, got = {}, 0
    for d in DIRS:
        dx, dy, dz = d
        if dz:
            src, count = z_at[dz] + (1 if dy < 0 else 0), 2 if dy == 0 else 1
        elif dy:
            src, count = y_at[dy] + (6 * narr if dx < 0 else 0), (8 if dx == 0 else 2) * narr
        else:
            src, count = x_at[dx], 6 * narr
        plan[d] = (src, got, count)
        got += count
    return plan, 28 * narr + 4, got


def plan1():
    plan, got = {}, 0
    for d in DIRS:
        dx, dy, dz = d
        if dz:
            src, count = 4, 1
        elif dx:
            src, count = (0 if dx > 0 else 2), 2
        else:
            src, count = 0, 4
        plan[d] = (src, got, count)
        got += count
    return plan, 5, got


PLAN2, SEND2, GOT2 = plan0(2)
PLANV, SENDV, GOTV = plan0(1)
PLAN1, SEND1, GOT1 = plan1()
GATHER = sorted(o for o in range(1, N) if o % 4 != 2)
SLOT = {o: i for i, o in enumerate(GATHER)}
SLOT[0] = len(GATHER)


def rows_of(shape):
    return lax.broadcasted_iota(jnp.int32, shape, len(shape) - 2)


def lanes_of(shape):
    return lax.broadcasted_iota(jnp.int32, shape, len(shape) - 1)


def rot(v, by, axis):
    by %= v.shape[axis]
    return pltpu.roll(v, by, axis) if by else v


def layer_loop(low, high, body, unroll=2):
    def step(x, carry):
        body(x)
        return carry

    lax.fori_loop(low, high, step, 0, unroll=unroll)


def start_to(me, src, dst, send, recv, off):
    pltpu.make_async_remote_copy(
        src_ref=src,
        dst_ref=dst,
        send_sem=send,
        recv_sem=recv,
        device_id={"space": lax.rem(me + (N - off) % N, N)},
        device_id_type=pl.DeviceIdType.MESH,
    ).start()


def send_plan(me, plan, sb, rb, send, recv):
    for d in sorted(plan, key=lambda d: -sum(map(abs, d))):
        src, got, count = plan[d]
        start_to(me, sb.at[pl.ds(src, count)], rb.at[pl.ds(got, count)], send, recv, offset(d))


def wait_got(rb, recv):
    pltpu.make_async_copy(rb, rb, recv).wait()


def wait_sent(rb, send):
    pltpu.make_async_copy(rb, rb, send).wait()


def pack0(own, narr, sb):
    x_at = {1: 0, -1: 6 * narr}
    y_at = {1: 12 * narr, -1: 20 * narr}
    z_at = {1: 28 * narr, -1: 28 * narr + 2}
    low4 = rows_of((8, 128)) < 4
    group = lanes_of((16, 128)) // 4
    zlo = zhi = jnp.zeros((16, 128), F32)
    for a in range(narr):
        for i in range(3):
            for side, x in ((1, i), (-1, 13 + i)):
                v = own(a, x)
                sb[x_at[side] + a * 6 + 2 * i] = v[0:8]
                sb[x_at[side] + a * 6 + 2 * i + 1] = v[8:16]
        for i in range(8):
            v, w = own(a, i), own(a, i + 8)
            sb[y_at[1] + i * narr + a] = jnp.where(low4, v[0:8], rot(w[0:8], 4, 0))
            sb[y_at[-1] + i * narr + a] = jnp.where(low4, rot(w[8:16], 4, 0), v[8:16])
        for x in range(16):
            v, g = own(a, x), 16 * a + x
            zlo = jnp.where(group == g, rot(v, 4 * g, 1), zlo)
            zhi = jnp.where(group == g, rot(v, 4 * g + 4, 1), zhi)
    for side, z in ((1, zlo), (-1, zhi)):
        sb[z_at[side]] = z[0:8]
        sb[z_at[side] + 1] = z[8:16]


def unpack0(a, narr, plan, rb, out):
    low4 = rows_of((8, 128)) < 4

    def at(d):
        return plan[d][1]

    for i in range(3):
        for dx, base in ((1, 20), (-1, 1)):
            first = at((dx, 0, 0)) + a * 6 + 2 * i
            out[base + i, 0:8, 0:128] = rb[first]
            out[base + i, 8:16, 0:128] = rb[first + 1]
    for i in range(8):
        up, lo = rb[at((0, 1, 0)) + i * narr + a], rb[at((0, -1, 0)) + i * narr + a]
        out[4 + i, 16:24, 0:128] = jnp.where(low4, up, lo)
        out[12 + i, 16:24, 0:128] = rot(jnp.where(low4, lo, up), 4, 0)
    for i in range(2):
        up, lo = rb[at((1, 1, 0)) + i * narr + a], rb[at((1, -1, 0)) + i * narr + a]
        out[20 + i, 16:24, 0:128] = jnp.where(low4, up, lo)
        up, lo = rb[at((-1, 1, 0)) + i * narr + a], rb[at((-1, -1, 0)) + i * narr + a]
        out[2 + i, 16:24, 0:128] = rot(jnp.where(low4, lo, up), 4, 0)
    half = lanes_of((24, 128)) < 64
    for dx, layers in ((0, range(4, 20)), (1, range(20, 23)), (-1, range(1, 4))):
        parts = {}
        for dz in (1, -1):
            mid = at((dx, 0, dz))
            tail = jnp.where(low4, rb[at((dx, 1, dz))], rb[at((dx, -1, dz))])
            parts[dz] = jnp.concatenate([rb[mid], rb[mid + 1], tail], axis=0)
        for x in layers:
            g = 16 * a + (x - 4) % 16
            out[x, :, 128:256] = jnp.where(half, rot(parts[1], -4 * g, 1), rot(parts[-1], 124 - 4 * g, 1))


def shifts0(ref, x):
    v = ref[x]
    return v, (
        ref[x - 1],
        ref[x + 1],
        pltpu.roll(v, 1, 0),
        pltpu.roll(v, 23, 0),
        pltpu.roll(v, 1, 1),
        pltpu.roll(v, 255, 1),
    )


def coefs_of(k, near):
    faces = [k + n for n in near]
    total = ((faces[0] + faces[1]) + (faces[2] + faces[3])) + (faces[4] + faces[5])
    inv = OMEGA / total
    return [f * inv for f in faces], 0.5 * total


def change(v, near, gs, c):
    t = [g * (n - v) for g, n in zip(gs, near)]
    return c + (((t[0] + t[1]) + (t[2] + t[3])) + (t[4] + t[5]))


def sweep0(cur, out, g, c, low, high):
    def body(x):
        v, near = shifts0(cur, x)
        out[x] = v + change(v, near, [g[i, x] for i in range(6)], c[x])

    layer_loop(low, high, body)


def own_residual0(cur, g, c, t, x):
    v, near = shifts0(cur, x)
    r = change(v, near, [g[i, x] for i in range(6)], c[x]) * t[x]
    return v, r[0:16, 0:128]


def pack1(w, sb):
    half = lanes_of((8, 128)) < 64
    lane = lanes_of((8, 128))
    for j in range(4):
        sb[j] = jnp.where(half, w[2 * j], w[2 * j + 1])
    z = jnp.zeros((8, 128), F32)
    for x in range(8):
        z = jnp.where(lane // 8 == 2 * x, rot(w[x], 16 * x, 1), z)
        z = jnp.where(lane // 8 == 2 * x + 1, rot(w[x], 16 * x + 8 - 60, 1), z)
    sb[4] = z


def unpack1(w, rb, out):
    half, quarter = lanes_of((8, 128)) < 64, lanes_of((8, 128)) < 96
    low4 = rows_of((8, 128)) < 4

    def block(dx, dy, x):
        if (dx, dy) == (0, 0):
            return w[x]
        first = 2 if dx < 0 else 0
        tile = rb[PLAN1[(dx, dy, 0)][1] + x // 2 - first]
        return rot(tile, 64, 1) if x % 2 else tile

    for dx, layers in ((0, range(8)), (1, range(4)), (-1, range(4, 8))):
        tail = {dz: rb[PLAN1[(dx, 0, dz)][1]] for dz in (1, -1)}
        tail1 = {
            dz: jnp.where(low4, rb[PLAN1[(dx, 1, dz)][1]], rb[PLAN1[(dx, -1, dz)][1]]) for dz in (1, -1)
        }
        for x in layers:
            ends = [jnp.where(quarter, rot(q[1], 64 - 16 * x, 1), rot(q[-1], 116 - 16 * x, 1)) for q in (tail, tail1)]
            out[4 + x + 8 * dx, 0:8] = jnp.where(half, block(dx, 0, x), ends[0])
            rows = jnp.where(low4, block(dx, 1, x), block(dx, -1, x))
            out[4 + x + 8 * dx, 8:16] = jnp.where(half, rows, ends[1])


def shifts1(ref, x):
    v = ref[x]
    return v, (
        ref[x - 1],
        ref[x + 1],
        pltpu.roll(v, 1, 0),
        pltpu.roll(v, 15, 0),
        pltpu.roll(v, 1, 1),
        pltpu.roll(v, 127, 1),
    )


def shifts_round(ref, x, step, lane_step):
    layers, rows = ref.shape[0], ref.shape[1]
    v = ref[x]
    row = rows_of(v.shape)
    below, above = ref[lax.rem(x + layers - step, layers)], ref[lax.rem(x + step, layers)]
    return v, (
        ref[lax.rem(x + layers - 1, layers)],
        ref[lax.rem(x + 1, layers)],
        pltpu.roll(jnp.where(row == rows - 1, below, v), 1, 0),
        pltpu.roll(jnp.where(row == 0, above, v), rows - 1, 0),
        pltpu.roll(v, lane_step, 1),
        pltpu.roll(v, 128 - lane_step, 1),
    )


def pack2(w2, sb):
    group = lanes_of((8, 128)) // 32
    z = w2[0]
    for x in range(1, 4):
        z = jnp.where(group == x, w2[x], z)
    sb[...] = z


def unpack2(rb, out):
    low4 = rows_of((8, 128)) < 4
    group = lanes_of((8, 128)) // 32
    for cx in range(4):
        for t in range(2):
            tiles = {}
            for dz in (-1, 0, 1):
                first = rb[SLOT[(16 * cx + 8 * t + dz) % N]]
                second = rb[SLOT[(16 * cx + 8 * t + 4 + dz) % N]]
                tiles[dz] = jnp.where(low4, first, second)
            for x in range(4):
                z = rot(tiles[0], -32 * x, 1)
                z = jnp.where(group == 1, rot(tiles[1], 32 - 32 * x, 1), z)
                z = jnp.where(group == 3, rot(tiles[-1], 96 - 32 * x, 1), z)
                out[4 * cx + x, 8 * t : 8 * t + 8] = z


def pair_rows(ref, index, count):
    return ref[index, pl.ds(0, count, stride=2), :] + ref[index, pl.ds(1, count, stride=2), :]


def kernel(
    cls_ref, val_ref, cell_ref, rate_ref, guess_ref, p_ref, r_ref,
    fr, vb, kf, g0, t0, c0, u0, sb2, rb2, sbv, rbv,
    pair, w1, k1, b1, v1, q1, g1, t1, c1, sbk1, rbk1, sbb1, rbb1, sbv1, rbv1,
    pair1, w2, k2, b2, v2, q2, g2, t2, c2, sbk2, rbk2, sbb2, rbb2,
    pair2, k3, v3, q3, g3, t3, c3, exp3, exp2, exp1, send, recv,
):
    me = lax.axis_index("space")
    barrier = pltpu.get_barrier_semaphore()
    for o in GATHER:
        pl.semaphore_signal(
            barrier, inc=1, device_id={"space": lax.rem(me + o, N)}, device_id_type=pl.DeviceIdType.MESH
        )

    def lookup(x):
        cls = cls_ref[0, x]
        b0, b1_, b2_ = (cls & 1) == 0, (cls & 2) == 0, (cls & 4) == 0
        pairs = [jnp.where(b0, val_ref[2 * i], val_ref[2 * i + 1]) for i in range(4)]
        quads = [jnp.where(b1_, pairs[0], pairs[1]), jnp.where(b1_, pairs[2], pairs[3])]
        kf[x + 4, 0:16, 0:128] = jnp.where(b2_, quads[0], quads[1])
        fr[x + 4, 0:16, 0:128] = guess_ref[0, x]

    layer_loop(0, 16, lookup)
    pack0(lambda a, x: (fr if a == 0 else kf)[x + 4, 0:16, 0:128], 2, sb2)

    pl.semaphore_wait(barrier, len(GATHER))
    send_plan(me, PLAN2, sb2, rb2, send.at[0], recv.at[0])

    def same(shape, f):
        return f(rows_of(shape), lanes_of(shape)).astype(F32)

    pool0 = same((128, 128), lambda l, c: l // 2 == c % 64)
    pool1 = same((128, 128), lambda l, c: (l // 2 == c % 32) & (l < 64))

    def coarsen0(layer):
        def body(x):
            pair[x] = layer(2 * x) + layer(2 * x + 1)

        layer_loop(0, 8, body, 1)
        sums = jnp.concatenate([pair_rows(pair, x, 8) for x in range(8)], axis=0)
        out = jnp.dot(0.125 * sums, pool0, precision=HI, preferred_element_type=F32)
        for x in range(8):
            w1[x] = out[8 * x : 8 * x + 8]

    def coarsen1(ref, base):
        for x in range(4):
            pair1[x] = ref[base + 2 * x] + ref[base + 2 * x + 1]
        rows = [pair_rows(pair1, x, 4) for x in range(4)]
        sums = jnp.concatenate([q for r in rows for q in (r, r)], axis=0)
        out = jnp.dot(0.125 * sums, pool1, precision=HI, preferred_element_type=F32)
        for x in range(4):
            w2[x] = out[8 * x : 8 * x + 8]

    even = lanes_of((8, 128)) % 2 == 0

    def coarsen2(ref, out):
        for x in range(8):
            pair2[x] = ref[2 * x] + ref[2 * x + 1]
        for x in range(8):
            s = 0.125 * pair_rows(pair2, x, 8)
            out[x] = s + jnp.where(even, pltpu.roll(s, 127, 1), pltpu.roll(s, 1, 1))

    coarsen0(lambda x: kf[x + 4, 0:16, 0:128])
    pack1(w1, sbk1)
    send_plan(me, PLAN1, sbk1, rbk1, send.at[1], recv.at[1])
    q1[0:8, 0:8] = w1[...]
    coarsen1(w1, 0)
    pack2(w2, sbk2)
    for o in GATHER:
        start_to(me, sbk2, rbk2.at[SLOT[o]], send.at[2], recv.at[2], o)

    cell, rate = cell_ref[...], rate_ref[...]
    ix, iy, iz = cell // (64 * 512), cell // 512 % 64, cell % 512
    theirs = (ix // 16 * 4 + iy // 16) * 4 + iz // 128
    place = lax.rem(theirs - lax.rem(me + ROTATE, N) + 2 * N + 21, N)
    dx, dy, dz = place // 16, place // 4 % 4, place % 4
    fx, fy, fz = ix % 16 + 16 * (dx - 1) + 4, iy % 16 + 16 * (dy - 1), iz % 128 + 128 * (dz - 1)
    held = (dx < 3) & (dy < 3) & (dz < 3) & (fy >= -4) & (fy < 20) & (fz >= -4) & (fz < 132)
    fy, fz = jnp.where(fy < 0, fy + 24, fy), jnp.where(fz < 0, fz + 256, fz)
    rate = jnp.where(held, rate, 0.0)
    in_y = jnp.where(rows_of((24, 16)) == fy, rate, 0.0)
    in_z = jnp.where(rows_of((256, 16)) == fz, 1.0, 0.0)
    left = jnp.concatenate([jnp.where(fx == x, in_y, 0.0) for x in range(24)], axis=0)
    c0[...] = lax.dot_general(
        left, in_z, (((1,), (1,)), ((), ())), precision=HI, preferred_element_type=F32
    ).reshape(24, 24, 256)

    wait_got(rb2, recv.at[0])
    unpack0(0, 2, PLAN2, rb2, fr)
    unpack0(1, 2, PLAN2, rb2, kf)

    def coefs0(x):
        k, near = shifts0(kf, x)
        gs, total = coefs_of(k, near)
        for i in range(6):
            g0[i, x] = gs[i]
        t0[x] = (1.0 / OMEGA) * total
        c0[x] = OMEGA * c0[x] / total

    layer_loop(2, 22, coefs0, 1)
    sweep0(fr, vb, g0, c0, 2, 22)
    sweep0(vb, u0, g0, c0, 3, 21)
    coarsen0(lambda x: own_residual0(u0, g0, c0, t0, x + 4)[1])
    pack1(w1, sbb1)
    send_plan(me, PLAN1, sbb1, rbb1, send.at[3], recv.at[3])
    pack0(lambda a, x: u0[x + 4, 0:16, 0:128], 1, sbv)
    send_plan(me, PLANV, sbv, rbv, send.at[4], recv.at[4])

    wait_got(rbk1, recv.at[1])
    unpack1(q1, rbk1, k1)

    def coefs1(x):
        k, near = shifts1(k1, x)
        gs, total = coefs_of(k, near)
        for i in range(6):
            g1[i, x] = gs[i]
        t1[x] = 0.25 * total

    layer_loop(1, 15, coefs1, 1)
    rbk2[SLOT[0]] = sbk2[...]
    wait_got(rbk2.at[pl.ds(0, len(GATHER))], recv.at[2])
    unpack2(rbk2, k2)
    outside = lanes_of((16, 128)) // 32 == 2

    def fill2(x):
        k2[x] = jnp.where(outside, 1.0, k2[x])

    layer_loop(0, 16, fill2)

    def coefs2(x):
        k, near = shifts_round(k2, x, 4, 1)
        gs, total = coefs_of(k, near)
        for i in range(6):
            g2[i, x] = gs[i]
        t2[x] = 0.0625 * total

    layer_loop(0, 16, coefs2, 1)
    coarsen2(k2, k3)

    def coefs3(x):
        k, near = shifts_round(k3, x, 2, 2)
        gs, total = coefs_of(k, near)
        for i in range(6):
            g3[i, x] = gs[i]
        t3[x] = 0.015625 * total

    layer_loop(0, 8, coefs3, 1)

    wait_got(rbb1, recv.at[3])
    unpack1(w1, rbb1, b1)

    def first1(x):
        c1[x] = OMEGA * b1[x] / t1[x]

    layer_loop(1, 15, first1)

    def sweep1(cur, out, low, high):
        def body(x):
            v, near = shifts1(cur, x)
            out[x] = v + change(v, near, [g1[i, x] for i in range(6)], c1[x])

        layer_loop(low, high, body)

    sweep1(c1, v1, 3, 13)

    def down1(x):
        v, near = shifts1(v1, x)
        r = change(v, near, [g1[i, x] for i in range(6)], c1[x]) * t1[x]
        q1[x] = (1.0 / OMEGA) * r[0:8]

    layer_loop(4, 12, down1)
    coarsen1(q1, 4)
    pack2(w2, sbb2)
    for o in GATHER:
        start_to(me, sbb2, rbb2.at[SLOT[o]], send.at[6], recv.at[6], o)
    half = lanes_of((8, 128)) < 64
    for x in range(8):
        v = v1[x + 4, 0:8]
        w1[x] = jnp.where(half, v, pltpu.roll(v, 64, 1))
    pack1(w1, sbv1)
    send_plan(me, PLAN1, sbv1, rbv1, send.at[5], recv.at[5])

    wait_sent(rb2, send.at[0])
    wait_sent(rbk1, send.at[1])
    wait_sent(rbk2.at[pl.ds(0, len(GATHER))], send.at[2])
    wait_sent(rbb1, send.at[3])
    wait_sent(rbv, send.at[4])
    wait_got(rbv, recv.at[4])
    unpack0(0, 1, PLANV, rbv, u0)
    wait_got(rbv1, recv.at[5])
    unpack1(w1, rbv1, v1)
    wait_sent(rbv1, send.at[5])

    rbb2[SLOT[0]] = sbb2[...]
    wait_got(rbb2.at[pl.ds(0, len(GATHER))], recv.at[6])
    unpack2(rbb2, b2)

    def first2(x):
        c2[x] = OMEGA * jnp.where(outside, 0.0, b2[x]) / t2[x]

    layer_loop(0, 16, first2)

    def sweep2(cur, out):
        def body(x):
            v, near = shifts_round(cur, x, 4, 1)
            out[x] = v + change(v, near, [g2[i, x] for i in range(6)], c2[x])

        layer_loop(0, 16, body)

    sweep2(c2, v2)

    def down2(x):
        v, near = shifts_round(v2, x, 4, 1)
        r = change(v, near, [g2[i, x] for i in range(6)], c2[x]) * t2[x]
        q2[x] = (1.0 / OMEGA) * r

    layer_loop(0, 16, down2)
    coarsen2(q2, c3)

    def first3(x):
        c3[x] = OMEGA * c3[x] / t3[x]

    layer_loop(0, 8, first3)

    def sweep3(cur, out):
        def body(x):
            v, near = shifts_round(cur, x, 2, 2)
            out[x] = v + change(v, near, [g3[i, x] for i in range(6)], c3[x])

        layer_loop(0, 8, body)

    sweep3(c3, v3)
    sweep3(v3, q3)
    sweep3(q3, v3)
    sweep3(v3, q3)
    sweep3(q3, v3)

    def up2(x):
        e = v3[x]
        exp3[x, pl.ds(0, 8, stride=2), :] = e
        exp3[x, pl.ds(1, 8, stride=2), :] = e
        q2[2 * x] = v2[2 * x] + exp3[x]
        q2[2 * x + 1] = v2[2 * x + 1] + exp3[x]

    layer_loop(0, 8, up2, 1)
    sweep2(q2, v2)
    sweep2(v2, q2)

    spread2 = same((128, 128), lambda c, f: c == jnp.where(f < 96, f // 2, 64 + f // 2))
    row = rows_of((8, 128))
    order = [14, 15, 0, 1, 2, 3, 4, 5]
    rows = [jnp.where(row < 6, q2[x, 0:8], q2[(x - 4) % 16, 8:16]) for x in order]
    out = jnp.dot(jnp.concatenate(rows, axis=0), spread2, precision=HI, preferred_element_type=F32)
    for i in range(8):
        e = out[8 * i : 8 * i + 8]
        exp2[i, pl.ds(0, 8, stride=2), :] = e
        exp2[i, pl.ds(1, 8, stride=2), :] = e
    for x in range(16):
        b1[x] = v1[x] + exp2[x // 2]
    sweep1(b1, v1, 1, 15)
    sweep1(v1, b1, 2, 14)

    def spread(c, f):
        return c == jnp.where(f < 192, f // 2, f // 2)

    spread1 = same((128, 256), spread)
    inside = (lanes_of((16, 128)) < 66) | (lanes_of((16, 128)) >= 126)
    rows = [jnp.where(inside, b1[x], 0.0) for x in range(2, 14)]
    out = jnp.dot(jnp.concatenate(rows, axis=0), spread1, precision=HI, preferred_element_type=F32)
    low4 = rows_of((8, 256)) < 4
    for i in range(12):
        for h in range(2):
            e = out[16 * i : 16 * i + 16, 128 * h : 128 * h + 128]
            exp1[i, h, pl.ds(0, 16, stride=2), :] = e
            exp1[i, h, pl.ds(1, 16, stride=2), :] = e
    low4 = rows_of((8, 128)) < 4
    for i in range(12):
        for h in range(2):
            tail = jnp.where(low4, exp1[i, h, 16:24], exp1[i, h, 24:32])
            for x in (2 * i, 2 * i + 1):
                if 1 <= x < 23:
                    at = pl.ds(128 * h, 128)
                    vb[x, 0:16, at] = u0[x, 0:16, at] + exp1[i, h, 0:16]
                    vb[x, 16:24, at] = u0[x, 16:24, at] + tail
    sweep0(vb, u0, g0, c0, 2, 22)
    sweep0(u0, vb, g0, c0, 3, 21)

    def finish(x):
        v, r = own_residual0(vb, g0, c0, t0, x + 4)
        p_ref[0, x] = v[0:16, 0:128]
        r_ref[0, x] = r

    layer_loop(0, 16, finish)
    wait_sent(rbb2.at[pl.ds(0, len(GATHER))], send.at[6])


def shards(perm_class, class_values, well_cells, well_rates, guess):
    wells = well_cells.shape[0]

    def f(*shape):
        return pltpu.VMEM(shape, F32)

    t = (8, 128)
    l0, l1, l2, l3 = (24, 24, 256), (16, 16, 128), (16, 16, 128), (8, 8, 128)
    vmem = pl.BlockSpec(memory_space=pltpu.VMEM)
    block = jax.ShapeDtypeStruct(guess.shape, F32)
    return pl.pallas_call(
        kernel,
        out_shape=(block, block),
        in_specs=[vmem, pl.BlockSpec(memory_space=pltpu.SMEM), vmem, vmem, vmem],
        out_specs=(vmem, vmem),
        scratch_shapes=[
            f(*l0), f(*l0), f(*l0), f(6, *l0), f(*l0), f(*l0), f(*l0),
            f(SEND2, *t), f(GOT2, *t), f(SENDV, *t), f(GOTV, *t),
            f(8, 16, 128), f(8, *t), f(*l1), f(*l1), f(*l1), f(16, *t), f(6, *l1), f(*l1), f(*l1),
            f(SEND1, *t), f(GOT1, *t), f(SEND1, *t), f(GOT1, *t), f(SEND1, *t), f(GOT1, *t),
            f(4, *t), f(4, *t), f(*l2), f(*l2), f(*l2), f(*l2), f(6, *l2), f(*l2), f(*l2),
            f(*t), f(len(GATHER) + 1, *t), f(*t), f(len(GATHER) + 1, *t),
            f(8, 16, 128), f(*l3), f(*l3), f(*l3), f(6, *l3), f(*l3), f(*l3),
            f(8, 16, 128), f(8, 16, 128), f(12, 2, 32, 128),
            pltpu.SemaphoreType.DMA((7,)), pltpu.SemaphoreType.DMA((7,)),
        ],
        compiler_params=pltpu.CompilerParams(
            collective_id=0, has_side_effects=True, vmem_limit_bytes=40 * 1024 * 1024
        ),
    )(perm_class, class_values, well_cells.reshape(1, wells), well_rates.reshape(1, wells), guess)


def solution(mesh):
    whole = P(("real", "space"), None, None, None)
    return jax.shard_map(
        shards,
        mesh=mesh,
        in_specs=(P("space", None, None, None), P(), P("real"), P("real"), whole),
        out_specs=(whole, whole),
        check_vma=False,
    )
```

```python
import functools

import jax
import jax.numpy as jnp
from jax import lax
from jax.experimental import pallas as pl
from jax.experimental.pallas import tpu as pltpu
from jax.sharding import PartitionSpec as P

N = 64
ROTATE = 21
OMEGA = 0.8
F32 = jnp.float32
HI = lax.Precision.HIGHEST
DIRS = [(a, b, c) for a in (-1, 0, 1) for b in (-1, 0, 1) for c in (-1, 0, 1) if (a, b, c) != (0, 0, 0)]


def offset(d):
    return (16 * d[0] + 4 * d[1] + d[2]) % N


def plan0(narr):
    x_at = {1: 0, -1: 6 * narr}
    y_at = {1: 12 * narr, -1: 20 * narr}
    z_at = {1: 28 * narr, -1: 28 * narr + 2}
    plan, got = {}, 0
    for d in DIRS:
        dx, dy, dz = d
        if dz:
            src, count = z_at[dz] + (1 if dy < 0 else 0), 2 if dy == 0 else 1
        elif dy:
            src, count = y_at[dy] + (6 * narr if dx < 0 else 0), (8 if dx == 0 else 2) * narr
        else:
            src, count = x_at[dx], 6 * narr
        plan[d] = (src, got, count)
        got += count
    return plan, 28 * narr + 4, got


def plan1():
    plan, got = {}, 0
    for d in DIRS:
        dx, dy, dz = d
        if dz:
            src, count = 4, 1
        elif dx:
            src, count = (0 if dx > 0 else 2), 2
        else:
            src, count = 0, 4
        plan[d] = (src, got, count)
        got += count
    return plan, 5, got


PLAN2, SEND2, GOT2 = plan0(2)
PLANV, SENDV, GOTV = plan0(1)
PLAN1, SEND1, GOT1 = plan1()
GATHER = sorted(o for o in range(1, N) if o % 4 != 2)
SLOT = {o: i for i, o in enumerate(GATHER)}
SLOT[0] = len(GATHER)


def rows_of(shape):
    return lax.broadcasted_iota(jnp.int32, shape, len(shape) - 2)


def lanes_of(shape):
    return lax.broadcasted_iota(jnp.int32, shape, len(shape) - 1)


def rot(v, by, axis):
    by %= v.shape[axis]
    return pltpu.roll(v, by, axis) if by else v


def layer_loop(low, high, body, unroll=None):
    def step(x, carry):
        body(x)
        return carry

    lax.fori_loop(low, high, step, 0, unroll=unroll or high - low)


def start_to(me, src, dst, send, recv, off):
    pltpu.make_async_remote_copy(
        src_ref=src,
        dst_ref=dst,
        send_sem=send,
        recv_sem=recv,
        device_id={"space": lax.rem(me + (N - off) % N, N)},
        device_id_type=pl.DeviceIdType.MESH,
    ).start()


def send_plan(me, plan, sb, rb, send, recv):
    for d in sorted(plan, key=lambda d: -sum(map(abs, d))):
        src, got, count = plan[d]
        start_to(me, sb.at[pl.ds(src, count)], rb.at[pl.ds(got, count)], send, recv, offset(d))


def wait_got(rb, recv):
    pltpu.make_async_copy(rb, rb, recv).wait()


def wait_sent(rb, send):
    pltpu.make_async_copy(rb, rb, send).wait()


def pack0(own, narr, sb):
    x_at = {1: 0, -1: 6 * narr}
    y_at = {1: 12 * narr, -1: 20 * narr}
    z_at = {1: 28 * narr, -1: 28 * narr + 2}
    low4 = rows_of((8, 128)) < 4
    group = lanes_of((16, 128)) // 4
    zlo = zhi = jnp.zeros((16, 128), F32)
    for a in range(narr):
        for i in range(3):
            for side, x in ((1, i), (-1, 13 + i)):
                v = own(a, x)
                sb[x_at[side] + a * 6 + 2 * i] = v[0:8]
                sb[x_at[side] + a * 6 + 2 * i + 1] = v[8:16]
        for i in range(8):
            v, w = own(a, i), own(a, i + 8)
            sb[y_at[1] + i * narr + a] = jnp.where(low4, v[0:8], rot(w[0:8], 4, 0))
            sb[y_at[-1] + i * narr + a] = jnp.where(low4, rot(w[8:16], 4, 0), v[8:16])
        for x in range(16):
            v, g = own(a, x), 16 * a + x
            zlo = jnp.where(group == g, rot(v, 4 * g, 1), zlo)
            zhi = jnp.where(group == g, rot(v, 4 * g + 4, 1), zhi)
    for side, z in ((1, zlo), (-1, zhi)):
        sb[z_at[side]] = z[0:8]
        sb[z_at[side] + 1] = z[8:16]


def unpack0(a, narr, plan, rb, out):
    low4 = rows_of((8, 128)) < 4

    def at(d):
        return plan[d][1]

    for i in range(3):
        for dx, base in ((1, 20), (-1, 1)):
            first = at((dx, 0, 0)) + a * 6 + 2 * i
            out[base + i, 0:8, 0:128] = rb[first]
            out[base + i, 8:16, 0:128] = rb[first + 1]
    for i in range(8):
        up, lo = rb[at((0, 1, 0)) + i * narr + a], rb[at((0, -1, 0)) + i * narr + a]
        out[4 + i, 16:24, 0:128] = jnp.where(low4, up, lo)
        out[12 + i, 16:24, 0:128] = rot(jnp.where(low4, lo, up), 4, 0)
    for i in range(2):
        up, lo = rb[at((1, 1, 0)) + i * narr + a], rb[at((1, -1, 0)) + i * narr + a]
        out[20 + i, 16:24, 0:128] = jnp.where(low4, up, lo)
        up, lo = rb[at((-1, 1, 0)) + i * narr + a], rb[at((-1, -1, 0)) + i * narr + a]
        out[2 + i, 16:24, 0:128] = rot(jnp.where(low4, lo, up), 4, 0)
    half = lanes_of((24, 128)) < 64
    for dx, layers in ((0, range(4, 20)), (1, range(20, 23)), (-1, range(1, 4))):
        parts = {}
        for dz in (1, -1):
            mid = at((dx, 0, dz))
            tail = jnp.where(low4, rb[at((dx, 1, dz))], rb[at((dx, -1, dz))])
            parts[dz] = jnp.concatenate([rb[mid], rb[mid + 1], tail], axis=0)
        for x in layers:
            g = 16 * a + (x - 4) % 16
            out[x, :, 128:256] = jnp.where(half, rot(parts[1], -4 * g, 1), rot(parts[-1], 124 - 4 * g, 1))


def shifts0(ref, x):
    v = ref[x]
    return v, (
        ref[x - 1],
        ref[x + 1],
        pltpu.roll(v, 1, 0),
        pltpu.roll(v, 23, 0),
        pltpu.roll(v, 1, 1),
        pltpu.roll(v, 255, 1),
    )


def coefs_of(k, near):
    faces = [k + n for n in near]
    total = ((faces[0] + faces[1]) + (faces[2] + faces[3])) + (faces[4] + faces[5])
    inv = OMEGA / total
    return [f * inv for f in faces], 0.5 * total


def change(v, near, gs, c):
    t = [g * (n - v) for g, n in zip(gs, near)]
    return c + (((t[0] + t[1]) + (t[2] + t[3])) + (t[4] + t[5]))


def sweep0(cur, out, g, c, low, high):
    def body(x):
        v, near = shifts0(cur, x)
        out[x] = v + change(v, near, [g[i, x] for i in range(6)], c[x])

    layer_loop(low, high, body)


def own_residual0(cur, g, c, t, x):
    v, near = shifts0(cur, x)
    r = change(v, near, [g[i, x] for i in range(6)], c[x]) * t[x]
    return v, r[0:16, 0:128]


def pack1(w, sb):
    half = lanes_of((8, 128)) < 64
    lane = lanes_of((8, 128))
    for j in range(4):
        sb[j] = jnp.where(half, w[2 * j], w[2 * j + 1])
    z = jnp.zeros((8, 128), F32)
    for x in range(8):
        z = jnp.where(lane // 8 == 2 * x, rot(w[x], 16 * x, 1), z)
        z = jnp.where(lane // 8 == 2 * x + 1, rot(w[x], 16 * x + 8 - 60, 1), z)
    sb[4] = z


def unpack1(w, rb, out):
    half, quarter = lanes_of((8, 128)) < 64, lanes_of((8, 128)) < 96
    low4 = rows_of((8, 128)) < 4

    def block(dx, dy, x):
        if (dx, dy) == (0, 0):
            return w[x]
        first = 2 if dx < 0 else 0
        tile = rb[PLAN1[(dx, dy, 0)][1] + x // 2 - first]
        return rot(tile, 64, 1) if x % 2 else tile

    for dx, layers in ((0, range(8)), (1, range(4)), (-1, range(4, 8))):
        tail = {dz: rb[PLAN1[(dx, 0, dz)][1]] for dz in (1, -1)}
        tail1 = {
            dz: jnp.where(low4, rb[PLAN1[(dx, 1, dz)][1]], rb[PLAN1[(dx, -1, dz)][1]]) for dz in (1, -1)
        }
        for x in layers:
            ends = [jnp.where(quarter, rot(q[1], 64 - 16 * x, 1), rot(q[-1], 116 - 16 * x, 1)) for q in (tail, tail1)]
            out[4 + x + 8 * dx, 0:8] = jnp.where(half, block(dx, 0, x), ends[0])
            rows = jnp.where(low4, block(dx, 1, x), block(dx, -1, x))
            out[4 + x + 8 * dx, 8:16] = jnp.where(half, rows, ends[1])


def shifts1(ref, x):
    v = ref[x]
    return v, (
        ref[x - 1],
        ref[x + 1],
        pltpu.roll(v, 1, 0),
        pltpu.roll(v, 15, 0),
        pltpu.roll(v, 1, 1),
        pltpu.roll(v, 127, 1),
    )


def shifts_round(ref, x, step, lane_step):
    layers, rows = ref.shape[0], ref.shape[1]
    v = ref[x]
    row = rows_of(v.shape)
    below, above = ref[lax.rem(x + layers - step, layers)], ref[lax.rem(x + step, layers)]
    return v, (
        ref[lax.rem(x + layers - 1, layers)],
        ref[lax.rem(x + 1, layers)],
        pltpu.roll(jnp.where(row == rows - 1, below, v), 1, 0),
        pltpu.roll(jnp.where(row == 0, above, v), rows - 1, 0),
        pltpu.roll(v, lane_step, 1),
        pltpu.roll(v, 128 - lane_step, 1),
    )


def pack2(w2, sb):
    group = lanes_of((8, 128)) // 32
    z = w2[0]
    for x in range(1, 4):
        z = jnp.where(group == x, w2[x], z)
    sb[...] = z


def unpack2(rb, out):
    low4 = rows_of((8, 128)) < 4
    group = lanes_of((8, 128)) // 32
    for cx in range(4):
        for t in range(2):
            tiles = {}
            for dz in (-1, 0, 1):
                first = rb[SLOT[(16 * cx + 8 * t + dz) % N]]
                second = rb[SLOT[(16 * cx + 8 * t + 4 + dz) % N]]
                tiles[dz] = jnp.where(low4, first, second)
            for x in range(4):
                z = rot(tiles[0], -32 * x, 1)
                z = jnp.where(group == 1, rot(tiles[1], 32 - 32 * x, 1), z)
                z = jnp.where(group == 3, rot(tiles[-1], 96 - 32 * x, 1), z)
                out[4 * cx + x, 8 * t : 8 * t + 8] = z


def pair_rows(ref, index, count):
    return ref[index, pl.ds(0, count, stride=2), :] + ref[index, pl.ds(1, count, stride=2), :]


def kernel(
    cls_ref, val_ref, cell_ref, rate_ref, guess_ref, p_ref, r_ref,
    fr, vb, kf, g0, t0, c0, u0, sb2, rb2, sbv, rbv,
    pair, w1, k1, b1, v1, q1, g1, t1, c1, sbk1, rbk1, sbb1, rbb1, sbv1, rbv1,
    pair1, w2, k2, b2, v2, q2, g2, t2, c2, sbk2, rbk2, sbb2, rbb2,
    pair2, k3, v3, q3, g3, t3, c3, exp3, exp2, exp1, send, recv,
):
    me = lax.axis_index("space")
    barrier = pltpu.get_barrier_semaphore()
    for o in GATHER:
        pl.semaphore_signal(
            barrier, inc=1, device_id={"space": lax.rem(me + o, N)}, device_id_type=pl.DeviceIdType.MESH
        )

    def lookup(x):
        cls = cls_ref[0, x]
        b0, b1_, b2_ = (cls & 1) == 0, (cls & 2) == 0, (cls & 4) == 0
        pairs = [jnp.where(b0, val_ref[2 * i], val_ref[2 * i + 1]) for i in range(4)]
        quads = [jnp.where(b1_, pairs[0], pairs[1]), jnp.where(b1_, pairs[2], pairs[3])]
        kf[x + 4, 0:16, 0:128] = jnp.where(b2_, quads[0], quads[1])
        fr[x + 4, 0:16, 0:128] = guess_ref[0, x]

    layer_loop(0, 16, lookup)
    pack0(lambda a, x: (fr if a == 0 else kf)[x + 4, 0:16, 0:128], 2, sb2)

    pl.semaphore_wait(barrier, len(GATHER))
    send_plan(me, PLAN2, sb2, rb2, send.at[0], recv.at[0])

    def same(shape, f):
        return f(rows_of(shape), lanes_of(shape)).astype(F32)

    pool0 = same((128, 128), lambda l, c: l // 2 == c % 64)
    pool1 = same((128, 128), lambda l, c: (l // 2 == c % 32) & (l < 64))

    def coarsen0(layer):
        def body(x):
            pair[x] = layer(2 * x) + layer(2 * x + 1)

        layer_loop(0, 8, body)
        sums = jnp.concatenate([pair_rows(pair, x, 8) for x in range(8)], axis=0)
        out = jnp.dot(0.125 * sums, pool0, precision=HI, preferred_element_type=F32)
        for x in range(8):
            w1[x] = out[8 * x : 8 * x + 8]

    def coarsen1(ref, base):
        for x in range(4):
            pair1[x] = ref[base + 2 * x] + ref[base + 2 * x + 1]
        rows = [pair_rows(pair1, x, 4) for x in range(4)]
        sums = jnp.concatenate([q for r in rows for q in (r, r)], axis=0)
        out = jnp.dot(0.125 * sums, pool1, precision=HI, preferred_element_type=F32)
        for x in range(4):
            w2[x] = out[8 * x : 8 * x + 8]

    even = lanes_of((8, 128)) % 2 == 0

    def coarsen2(ref, out):
        for x in range(8):
            pair2[x] = ref[2 * x] + ref[2 * x + 1]
        for x in range(8):
            s = 0.125 * pair_rows(pair2, x, 8)
            out[x] = s + jnp.where(even, pltpu.roll(s, 127, 1), pltpu.roll(s, 1, 1))

    coarsen0(lambda x: kf[x + 4, 0:16, 0:128])
    pack1(w1, sbk1)
    send_plan(me, PLAN1, sbk1, rbk1, send.at[1], recv.at[1])
    q1[0:8, 0:8] = w1[...]
    coarsen1(w1, 0)
    pack2(w2, sbk2)
    for o in GATHER:
        start_to(me, sbk2, rbk2.at[SLOT[o]], send.at[2], recv.at[2], o)

    cell, rate = cell_ref[...], rate_ref[...]
    ix, iy, iz = cell // (64 * 512), cell // 512 % 64, cell % 512
    theirs = (ix // 16 * 4 + iy // 16) * 4 + iz // 128
    place = lax.rem(theirs - lax.rem(me + ROTATE, N) + 2 * N + 21, N)
    dx, dy, dz = place // 16, place // 4 % 4, place % 4
    fx, fy, fz = ix % 16 + 16 * (dx - 1) + 4, iy % 16 + 16 * (dy - 1), iz % 128 + 128 * (dz - 1)
    held = (dx < 3) & (dy < 3) & (dz < 3) & (fy >= -4) & (fy < 20) & (fz >= -4) & (fz < 132)
    fy, fz = jnp.where(fy < 0, fy + 24, fy), jnp.where(fz < 0, fz + 256, fz)
    rate = jnp.where(held, rate, 0.0)
    in_y = jnp.where(rows_of((24, 16)) == fy, rate, 0.0)
    in_z = jnp.where(rows_of((256, 16)) == fz, 1.0, 0.0)
    left = jnp.concatenate([jnp.where(fx == x, in_y, 0.0) for x in range(24)], axis=0)
    c0[...] = lax.dot_general(
        left, in_z, (((1,), (1,)), ((), ())), precision=HI, preferred_element_type=F32
    ).reshape(24, 24, 256)

    wait_got(rb2, recv.at[0])
    unpack0(0, 2, PLAN2, rb2, fr)
    unpack0(1, 2, PLAN2, rb2, kf)

    def coefs0(x):
        k, near = shifts0(kf, x)
        gs, total = coefs_of(k, near)
        for i in range(6):
            g0[i, x] = gs[i]
        t0[x] = (1.0 / OMEGA) * total
        c0[x] = OMEGA * c0[x] / total

    layer_loop(2, 22, coefs0)
    sweep0(fr, vb, g0, c0, 2, 22)
    sweep0(vb, u0, g0, c0, 3, 21)
    coarsen0(lambda x: own_residual0(u0, g0, c0, t0, x + 4)[1])
    pack1(w1, sbb1)
    send_plan(me, PLAN1, sbb1, rbb1, send.at[3], recv.at[3])
    pack0(lambda a, x: u0[x + 4, 0:16, 0:128], 1, sbv)
    send_plan(me, PLANV, sbv, rbv, send.at[4], recv.at[4])

    wait_got(rbk1, recv.at[1])
    unpack1(q1, rbk1, k1)

    def coefs1(x):
        k, near = shifts1(k1, x)
        gs, total = coefs_of(k, near)
        for i in range(6):
            g1[i, x] = gs[i]
        t1[x] = 0.25 * total

    layer_loop(1, 15, coefs1)
    rbk2[SLOT[0]] = sbk2[...]
    wait_got(rbk2.at[pl.ds(0, len(GATHER))], recv.at[2])
    unpack2(rbk2, k2)
    outside = lanes_of((16, 128)) // 32 == 2

    def fill2(x):
        k2[x] = jnp.where(outside, 1.0, k2[x])

    layer_loop(0, 16, fill2)

    def coefs2(x):
        k, near = shifts_round(k2, x, 4, 1)
        gs, total = coefs_of(k, near)
        for i in range(6):
            g2[i, x] = gs[i]
        t2[x] = 0.0625 * total

    layer_loop(0, 16, coefs2)
    coarsen2(k2, k3)

    def coefs3(x):
        k, near = shifts_round(k3, x, 2, 2)
        gs, total = coefs_of(k, near)
        for i in range(6):
            g3[i, x] = gs[i]
        t3[x] = 0.015625 * total

    layer_loop(0, 8, coefs3)

    wait_got(rbb1, recv.at[3])
    unpack1(w1, rbb1, b1)

    def first1(x):
        c1[x] = OMEGA * b1[x] / t1[x]

    layer_loop(1, 15, first1)

    def sweep1(cur, out, low, high):
        def body(x):
            v, near = shifts1(cur, x)
            out[x] = v + change(v, near, [g1[i, x] for i in range(6)], c1[x])

        layer_loop(low, high, body)

    sweep1(c1, v1, 3, 13)

    def down1(x):
        v, near = shifts1(v1, x)
        r = change(v, near, [g1[i, x] for i in range(6)], c1[x]) * t1[x]
        q1[x] = (1.0 / OMEGA) * r[0:8]

    layer_loop(4, 12, down1)
    coarsen1(q1, 4)
    pack2(w2, sbb2)
    for o in GATHER:
        start_to(me, sbb2, rbb2.at[SLOT[o]], send.at[6], recv.at[6], o)
    half = lanes_of((8, 128)) < 64
    for x in range(8):
        v = v1[x + 4, 0:8]
        w1[x] = jnp.where(half, v, pltpu.roll(v, 64, 1))
    pack1(w1, sbv1)
    send_plan(me, PLAN1, sbv1, rbv1, send.at[5], recv.at[5])

    wait_sent(rb2, send.at[0])
    wait_sent(rbk1, send.at[1])
    wait_sent(rbk2.at[pl.ds(0, len(GATHER))], send.at[2])
    wait_sent(rbb1, send.at[3])
    wait_sent(rbv, send.at[4])
    wait_got(rbv, recv.at[4])
    unpack0(0, 1, PLANV, rbv, u0)
    wait_got(rbv1, recv.at[5])
    unpack1(w1, rbv1, v1)
    wait_sent(rbv1, send.at[5])

    rbb2[SLOT[0]] = sbb2[...]
    wait_got(rbb2.at[pl.ds(0, len(GATHER))], recv.at[6])
    unpack2(rbb2, b2)

    def first2(x):
        c2[x] = OMEGA * jnp.where(outside, 0.0, b2[x]) / t2[x]

    layer_loop(0, 16, first2)

    def sweep2(cur, out):
        def body(x):
            v, near = shifts_round(cur, x, 4, 1)
            out[x] = v + change(v, near, [g2[i, x] for i in range(6)], c2[x])

        layer_loop(0, 16, body)

    sweep2(c2, v2)

    def down2(x):
        v, near = shifts_round(v2, x, 4, 1)
        r = change(v, near, [g2[i, x] for i in range(6)], c2[x]) * t2[x]
        q2[x] = (1.0 / OMEGA) * r

    layer_loop(0, 16, down2)
    coarsen2(q2, c3)

    def first3(x):
        c3[x] = OMEGA * c3[x] / t3[x]

    layer_loop(0, 8, first3)

    def sweep3(cur, out):
        def body(x):
            v, near = shifts_round(cur, x, 2, 2)
            out[x] = v + change(v, near, [g3[i, x] for i in range(6)], c3[x])

        layer_loop(0, 8, body)

    sweep3(c3, v3)
    sweep3(v3, q3)
    sweep3(q3, v3)
    sweep3(v3, q3)
    sweep3(q3, v3)

    def up2(x):
        e = v3[x]
        exp3[x, pl.ds(0, 8, stride=2), :] = e
        exp3[x, pl.ds(1, 8, stride=2), :] = e
        q2[2 * x] = v2[2 * x] + exp3[x]
        q2[2 * x + 1] = v2[2 * x + 1] + exp3[x]

    layer_loop(0, 8, up2)
    sweep2(q2, v2)
    sweep2(v2, q2)

    spread2 = same((128, 128), lambda c, f: c == jnp.where(f < 96, f // 2, 64 + f // 2))
    row = rows_of((8, 128))
    order = [14, 15, 0, 1, 2, 3, 4, 5]
    rows = [jnp.where(row < 6, q2[x, 0:8], q2[(x - 4) % 16, 8:16]) for x in order]
    out = jnp.dot(jnp.concatenate(rows, axis=0), spread2, precision=HI, preferred_element_type=F32)
    for i in range(8):
        e = out[8 * i : 8 * i + 8]
        exp2[i, pl.ds(0, 8, stride=2), :] = e
        exp2[i, pl.ds(1, 8, stride=2), :] = e
    for x in range(16):
        b1[x] = v1[x] + exp2[x // 2]
    sweep1(b1, v1, 1, 15)
    sweep1(v1, b1, 2, 14)

    def spread(c, f):
        return c == jnp.where(f < 192, f // 2, f // 2)

    spread1 = same((128, 256), spread)
    inside = (lanes_of((16, 128)) < 66) | (lanes_of((16, 128)) >= 126)
    rows = [jnp.where(inside, b1[x], 0.0) for x in range(2, 14)]
    out = jnp.dot(jnp.concatenate(rows, axis=0), spread1, precision=HI, preferred_element_type=F32)
    low4 = rows_of((8, 256)) < 4
    for i in range(12):
        for h in range(2):
            e = out[16 * i : 16 * i + 16, 128 * h : 128 * h + 128]
            exp1[i, h, pl.ds(0, 16, stride=2), :] = e
            exp1[i, h, pl.ds(1, 16, stride=2), :] = e
    low4 = rows_of((8, 128)) < 4
    for i in range(12):
        for h in range(2):
            tail = jnp.where(low4, exp1[i, h, 16:24], exp1[i, h, 24:32])
            for x in (2 * i, 2 * i + 1):
                if 1 <= x < 23:
                    at = pl.ds(128 * h, 128)
                    vb[x, 0:16, at] = u0[x, 0:16, at] + exp1[i, h, 0:16]
                    vb[x, 16:24, at] = u0[x, 16:24, at] + tail
    sweep0(vb, u0, g0, c0, 2, 22)
    sweep0(u0, vb, g0, c0, 3, 21)

    def finish(x):
        v, r = own_residual0(vb, g0, c0, t0, x + 4)
        p_ref[0, x] = v[0:16, 0:128]
        r_ref[0, x] = r

    layer_loop(0, 16, finish)
    wait_sent(rbb2.at[pl.ds(0, len(GATHER))], send.at[6])


def shards(perm_class, class_values, well_cells, well_rates, guess):
    wells = well_cells.shape[0]

    def f(*shape):
        return pltpu.VMEM(shape, F32)

    t = (8, 128)
    l0, l1, l2, l3 = (24, 24, 256), (16, 16, 128), (16, 16, 128), (8, 8, 128)
    vmem = pl.BlockSpec(memory_space=pltpu.VMEM)
    block = jax.ShapeDtypeStruct(guess.shape, F32)
    return pl.pallas_call(
        kernel,
        out_shape=(block, block),
        in_specs=[vmem, pl.BlockSpec(memory_space=pltpu.SMEM), vmem, vmem, vmem],
        out_specs=(vmem, vmem),
        scratch_shapes=[
            f(*l0), f(*l0), f(*l0), f(6, *l0), f(*l0), f(*l0), f(*l0),
            f(SEND2, *t), f(GOT2, *t), f(SENDV, *t), f(GOTV, *t),
            f(8, 16, 128), f(8, *t), f(*l1), f(*l1), f(*l1), f(16, *t), f(6, *l1), f(*l1), f(*l1),
            f(SEND1, *t), f(GOT1, *t), f(SEND1, *t), f(GOT1, *t), f(SEND1, *t), f(GOT1, *t),
            f(4, *t), f(4, *t), f(*l2), f(*l2), f(*l2), f(*l2), f(6, *l2), f(*l2), f(*l2),
            f(*t), f(len(GATHER) + 1, *t), f(*t), f(len(GATHER) + 1, *t),
            f(8, 16, 128), f(*l3), f(*l3), f(*l3), f(6, *l3), f(*l3), f(*l3),
            f(8, 16, 128), f(8, 16, 128), f(12, 2, 32, 128),
            pltpu.SemaphoreType.DMA((7,)), pltpu.SemaphoreType.DMA((7,)),
        ],
        compiler_params=pltpu.CompilerParams(
            collective_id=0, has_side_effects=True, vmem_limit_bytes=40 * 1024 * 1024
        ),
    )(perm_class, class_values, well_cells.reshape(1, wells), well_rates.reshape(1, wells), guess)


def solution(mesh):
    whole = P(("real", "space"), None, None, None)
    return jax.shard_map(
        shards,
        mesh=mesh,
        in_specs=(P("space", None, None, None), P(), P("real"), P("real"), whole),
        out_specs=(whole, whole),
        check_vma=False,
    )
```

```python
import functools

import jax
import jax.numpy as jnp
from jax import lax
from jax.experimental import pallas as pl
from jax.experimental.pallas import tpu as pltpu
from jax.sharding import PartitionSpec as P

N = 64
ROTATE = 21
OMEGA = 0.8
F32 = jnp.float32
HI = lax.Precision.HIGHEST
DIRS = [(a, b, c) for a in (-1, 0, 1) for b in (-1, 0, 1) for c in (-1, 0, 1) if (a, b, c) != (0, 0, 0)]


def offset(d):
    return (16 * d[0] + 4 * d[1] + d[2]) % N


def hops(off):
    total = 0
    for row in range(N):
        to = (row + off) % N
        y, z = abs(row // 16 - to // 16), abs(row // 2 % 8 - to // 2 % 8)
        total += min(y, 4 - y) + min(z, 8 - z) + 2 * abs(row % 2 - to % 2)
    return total


def sent0(narr):
    x_at = {1: 0, -1: 6 * narr}
    y_at = {1: 12 * narr, -1: 20 * narr}
    e_at = {d: 28 * narr + i for i, d in enumerate([(1, 1), (1, -1), (-1, 1), (-1, -1)])}
    z_at = {1: 28 * narr + 4, -1: 28 * narr + 6}
    return x_at, y_at, e_at, z_at, 28 * narr + 8


def plan0(narr):
    x_at, y_at, e_at, z_at, length = sent0(narr)
    plan, got = {}, 0
    for d in DIRS:
        dx, dy, dz = d
        if dz:
            src, count = z_at[dz] + (1 if dy < 0 else 0), 2 if dy == 0 else 1
        elif dx and dy:
            src, count = e_at[(dx, dy)], 1
        elif dy:
            src, count = y_at[dy], 8 * narr
        else:
            src, count = x_at[dx], 6 * narr
        plan[d] = (src, got, count)
        got += count
    return plan, length, got


def plan1(narr):
    plan, got = {}, 0
    for d in DIRS:
        dx, dy, dz = d
        if dz:
            src, count = 8 * narr, 1
        elif dy:
            src = (4 if dy > 0 else 6) * narr + (narr if dx < 0 else 0)
            count = narr if dx else 2 * narr
        else:
            src, count = (0 if dx > 0 else 2 * narr), 2 * narr
        plan[d] = (src, got, count)
        got += count
    return plan, 8 * narr + 1, got


PLAN2, SEND2, GOT2 = plan0(2)
PLANV, SENDV, GOTV = plan0(1)
PLANS1 = {n: plan1(n) for n in (1, 2)}
NEAR = sorted((offset(d) for d in DIRS), key=lambda o: (-hops(o), o))
GATHER = sorted((o for o in range(1, N) if o % 4 != 2), key=lambda o: (-hops(o), o))
SLOT = {o: i for i, o in enumerate(GATHER)}
SLOT[0] = len(GATHER)


def rows_of(shape):
    return lax.broadcasted_iota(jnp.int32, shape, len(shape) - 2)


def lanes_of(shape):
    return lax.broadcasted_iota(jnp.int32, shape, len(shape) - 1)


def rot(v, by, axis):
    by %= v.shape[axis]
    return pltpu.roll(v, by, axis) if by else v


def layer_loop(low, high, body, unroll=None):
    def step(x, carry):
        body(x)
        return carry

    lax.fori_loop(low, high, step, 0, unroll=unroll or high - low)


def start_to(me, src, dst, send, recv, off):
    pltpu.make_async_remote_copy(
        src_ref=src,
        dst_ref=dst,
        send_sem=send,
        recv_sem=recv,
        device_id={"space": lax.rem(me + (N - off) % N, N)},
        device_id_type=pl.DeviceIdType.MESH,
    ).start()


def send_plan(me, plan, sb, rb, send, recv):
    for d in sorted(plan, key=lambda d: -hops(offset(d))):
        src, got, count = plan[d]
        start_to(me, sb.at[pl.ds(src, count)], rb.at[pl.ds(got, count)], send, recv, offset(d))


def wait_got(rb, recv):
    pltpu.make_async_copy(rb, rb, recv).wait()


def wait_sent(rb, send):
    pltpu.make_async_copy(rb, rb, send).wait()


def pack0(own, narr, sb):
    x_at, y_at, e_at, z_at, _ = sent0(narr)
    low4 = rows_of((8, 128)) < 4
    two = rows_of((8, 128)) // 2
    group = lanes_of((16, 128)) // 4
    zlo = zhi = jnp.zeros((16, 128), F32)
    for a in range(narr):
        for i in range(3):
            for side, x in ((1, i), (-1, 13 + i)):
                v = own(a, x)
                sb[x_at[side] + a * 6 + 2 * i] = v[0:8]
                sb[x_at[side] + a * 6 + 2 * i + 1] = v[8:16]
        for i in range(8):
            v, w = own(a, i), own(a, i + 8)
            sb[y_at[1] + i * narr + a] = jnp.where(low4, v[0:8], rot(w[0:8], 4, 0))
            sb[y_at[-1] + i * narr + a] = jnp.where(low4, rot(w[8:16], 4, 0), v[8:16])
    for (dx, dy), at in e_at.items():
        z = jnp.zeros((8, 128), F32)
        for a in range(narr):
            for i in range(2):
                v = own(a, i if dx > 0 else 14 + i)
                v = v[0:8] if dy > 0 else v[8:16]
                z = jnp.where(two == 2 * a + i, rot(v, 4 * a + 2 * i - (0 if dy > 0 else 6), 0), z)
        sb[at] = z
    for a in range(narr):
        for x in range(16):
            v, g = own(a, x), 16 * a + x
            zlo = jnp.where(group == g, rot(v, 4 * g, 1), zlo)
            zhi = jnp.where(group == g, rot(v, 4 * g + 4, 1), zhi)
    for side, z in ((1, zlo), (-1, zhi)):
        sb[z_at[side]] = z[0:8]
        sb[z_at[side] + 1] = z[8:16]


def unpack0(a, narr, plan, rb, out):
    low4 = rows_of((8, 128)) < 4

    def at(d):
        return plan[d][1]

    for i in range(3):
        for dx, base in ((1, 20), (-1, 1)):
            first = at((dx, 0, 0)) + a * 6 + 2 * i
            out[base + i, 0:8, 0:128] = rb[first]
            out[base + i, 8:16, 0:128] = rb[first + 1]
    for i in range(8):
        up, lo = rb[at((0, 1, 0)) + i * narr + a], rb[at((0, -1, 0)) + i * narr + a]
        out[4 + i, 16:24, 0:128] = jnp.where(low4, up, lo)
        out[12 + i, 16:24, 0:128] = rot(jnp.where(low4, lo, up), 4, 0)
    for dx, base in ((1, 20), (-1, 2)):
        for i in range(2):
            up = rot(rb[at((dx, 1, 0))], -(4 * a + 2 * i), 0)
            lo = rot(rb[at((dx, -1, 0))], 6 - (4 * a + 2 * i), 0)
            out[base + i, 16:24, 0:128] = jnp.where(low4, up, lo)
    half = lanes_of((24, 128)) < 64
    for dx, layers in ((0, range(4, 20)), (1, range(20, 23)), (-1, range(1, 4))):
        parts = {}
        for dz in (1, -1):
            mid = at((dx, 0, dz))
            tail = jnp.where(low4, rb[at((dx, 1, dz))], rb[at((dx, -1, dz))])
            parts[dz] = jnp.concatenate([rb[mid], rb[mid + 1], tail], axis=0)
        for x in layers:
            g = 16 * a + (x - 4) % 16
            out[x, :, 128:256] = jnp.where(half, rot(parts[1], -4 * g, 1), rot(parts[-1], 124 - 4 * g, 1))


def shifts0(ref, x):
    v = ref[x]
    return v, (
        ref[x - 1],
        ref[x + 1],
        pltpu.roll(v, 1, 0),
        pltpu.roll(v, 23, 0),
        pltpu.roll(v, 1, 1),
        pltpu.roll(v, 255, 1),
    )


def coefs_of(k, near):
    faces = [k + n for n in near]
    total = ((faces[0] + faces[1]) + (faces[2] + faces[3])) + (faces[4] + faces[5])
    inv = OMEGA / total
    return [f * inv for f in faces], 0.5 * total


def change(v, near, gs, c):
    t = [g * (n - v) for g, n in zip(gs, near)]
    return c + (((t[0] + t[1]) + (t[2] + t[3])) + (t[4] + t[5]))


def sweep0(cur, out, g, c, low, high):
    def body(x):
        v, near = shifts0(cur, x)
        out[x] = v + change(v, near, [g[i, x] for i in range(6)], c[x])

    layer_loop(low, high, body)


def own_residual0(cur, g, c, t, x):
    v, near = shifts0(cur, x)
    r = change(v, near, [g[i, x] for i in range(6)], c[x]) * t[x]
    return v, r[0:16, 0:128]


def pack1(ws, sb):
    narr = len(ws)
    half, low4 = lanes_of((8, 128)) < 64, rows_of((8, 128)) < 4
    group = lanes_of((8, 128)) // 4
    z = jnp.zeros((8, 128), F32)
    for a, w in enumerate(ws):
        for j in range(4):
            sb[j * narr + a] = jnp.where(half, w[2 * j], w[2 * j + 1])
        for j in range(2):
            p, q, r, t = (w[4 * j + i] for i in range(4))
            here, there = jnp.where(half, p, r), rot(jnp.where(half, q, t), 4, 0)
            sb[(4 + j) * narr + a] = jnp.where(low4, here, there)
            sb[(6 + j) * narr + a] = jnp.where(low4, there, here)
        for x in range(8):
            g = 16 * a + x
            z = jnp.where(group == g, rot(w[x], 4 * g, 1), z)
            z = jnp.where(group == g + 8, rot(w[x], 4 * (g + 8) - 60, 1), z)
    sb[8 * narr] = z


def unpack1(a, narr, w, rb, out):
    half, quarter = lanes_of((8, 128)) < 64, lanes_of((8, 128)) < 96
    low4 = rows_of((8, 128)) < 4
    plan = PLANS1[narr][0]

    def at(d, j=0):
        return rb[plan[d][1] + j * narr + a]

    def layer(dx, x):
        if dx == 0:
            return w[x]
        tile = at((dx, 0, 0), x // 2 - (2 if dx < 0 else 0))
        return rot(tile, 64, 1) if x % 2 else tile

    def rows(dx, x):
        j = x // 4 if dx == 0 else 0
        up, lo = at((dx, 1, 0), j), at((dx, -1, 0), j)
        tile = rot(jnp.where(low4, lo, up), 4, 0) if x % 2 else jnp.where(low4, up, lo)
        return rot(tile, 64, 1) if x % 4 > 1 else tile

    for dx, layers in ((0, range(8)), (1, range(4)), (-1, range(4, 8))):
        tail = {dz: rb[plan[(dx, 0, dz)][1]] for dz in (1, -1)}
        tail1 = {dz: jnp.where(low4, rb[plan[(dx, 1, dz)][1]], rb[plan[(dx, -1, dz)][1]]) for dz in (1, -1)}
        for x in layers:
            g = 16 * a + x
            ends = [jnp.where(quarter, rot(q[1], 64 - 4 * g, 1), rot(q[-1], 124 - 4 * (g + 8), 1)) for q in (tail, tail1)]
            out[4 + x + 8 * dx, 0:8] = jnp.where(half, layer(dx, x), ends[0])
            out[4 + x + 8 * dx, 8:16] = jnp.where(half, rows(dx, x), ends[1])


def shifts1(ref, x):
    v = ref[x]
    return v, (
        ref[x - 1],
        ref[x + 1],
        pltpu.roll(v, 1, 0),
        pltpu.roll(v, 15, 0),
        pltpu.roll(v, 1, 1),
        pltpu.roll(v, 127, 1),
    )


def shifts_round(ref, x, step, lane_step):
    layers, rows = ref.shape[0], ref.shape[1]
    v = ref[x]
    row = rows_of(v.shape)
    below, above = ref[lax.rem(x + layers - step, layers)], ref[lax.rem(x + step, layers)]
    return v, (
        ref[lax.rem(x + layers - 1, layers)],
        ref[lax.rem(x + 1, layers)],
        pltpu.roll(jnp.where(row == rows - 1, below, v), 1, 0),
        pltpu.roll(jnp.where(row == 0, above, v), rows - 1, 0),
        pltpu.roll(v, lane_step, 1),
        pltpu.roll(v, 128 - lane_step, 1),
    )


def pack2(w2, sb):
    group = lanes_of((8, 128)) // 32
    z = w2[0]
    for x in range(1, 4):
        z = jnp.where(group == x, w2[x], z)
    sb[...] = z[0:4]


def unpack2(rb, out):
    group = lanes_of((8, 128)) // 32
    for cx in range(4):
        for t in range(2):
            tiles = {}
            for dz in (-1, 0, 1):
                first = rb[SLOT[(16 * cx + 8 * t + dz) % N]]
                second = rb[SLOT[(16 * cx + 8 * t + 4 + dz) % N]]
                tiles[dz] = jnp.concatenate([first, second], axis=0)
            for x in range(4):
                z = rot(tiles[0], -32 * x, 1)
                z = jnp.where(group == 1, rot(tiles[1], 32 - 32 * x, 1), z)
                z = jnp.where(group == 3, rot(tiles[-1], 96 - 32 * x, 1), z)
                out[4 * cx + x, 8 * t : 8 * t + 8] = z


def pair_rows(ref, index, count):
    return ref[index, pl.ds(0, count, stride=2), :] + ref[index, pl.ds(1, count, stride=2), :]


def kernel(
    cls_hbm, val_hbm, cell_hbm, rate_hbm, guess_hbm, p_ref, r_ref,
    cls_ref, val_ref, cell_ref, rate_ref, fr, vb, kf, g0, t0, c0, u0, sb2, rb2, sbv, rbv,
    pair, w1, wk, k1, b1, v1, q1, g1, t1, c1, sbb1, rbb1, sbv1, rbv1,
    pair1, w2, k2, b2, v2, q2, g2, t2, c2, sbk2, rbk2, sbb2, rbb2,
    pair2, k3, v3, q3, g3, t3, c3, exp3, exp2, exp1, send, recv, load,
):
    me = lax.axis_index("space")
    loads = [
        pltpu.make_async_copy(src, dst, load.at[i])
        for i, (src, dst) in enumerate(
            [
                (cls_hbm.at[0], cls_ref),
                (val_hbm, val_ref),
                (guess_hbm.at[0], fr.at[pl.ds(4, 16), pl.ds(0, 16), pl.ds(0, 128)]),
                (cell_hbm, cell_ref),
                (rate_hbm, rate_ref),
            ]
        )
    ]
    for copy in loads:
        copy.start()
    barrier = pltpu.get_barrier_semaphore()
    for o in NEAR:
        pl.semaphore_signal(
            barrier, inc=1, device_id={"space": lax.rem(me + o, N)}, device_id_type=pl.DeviceIdType.MESH
        )

    for copy in loads:
        copy.wait()
    vals = [jnp.broadcast_to(val_ref[0:1, i : i + 1], (16, 128)) for i in range(8)]

    def lookup(x):
        cls = cls_ref[x]
        bits = [(cls & 1) == 0, (cls & 2) == 0, (cls & 4) == 0]
        pairs = [jnp.where(bits[0], vals[2 * i], vals[2 * i + 1]) for i in range(4)]
        quads = [jnp.where(bits[1], pairs[0], pairs[1]), jnp.where(bits[1], pairs[2], pairs[3])]
        kf[x + 4, 0:16, 0:128] = jnp.where(bits[2], quads[0], quads[1])

    layer_loop(0, 16, lookup)
    pack0(lambda a, x: (fr if a == 0 else kf)[x + 4, 0:16, 0:128], 2, sb2)
    pl.semaphore_wait(barrier, len(NEAR))
    send_plan(me, PLAN2, sb2, rb2, send.at[0], recv.at[0])

    def same(shape, f):
        return f(rows_of(shape), lanes_of(shape)).astype(F32)

    pool0 = same((128, 128), lambda l, c: l // 2 == c % 64)
    pool1 = same((128, 128), lambda l, c: (l // 2 == c % 32) & (l < 64))

    def coarsen0(layer, w1):
        def body(x):
            pair[x] = layer(2 * x) + layer(2 * x + 1)

        layer_loop(0, 8, body)
        sums = jnp.concatenate([pair_rows(pair, x, 8) for x in range(8)], axis=0)
        out = jnp.dot(0.125 * sums, pool0, precision=HI, preferred_element_type=F32)
        for x in range(8):
            w1[x] = out[8 * x : 8 * x + 8]

    def coarsen1(ref, base):
        for x in range(4):
            pair1[x] = ref[base + 2 * x] + ref[base + 2 * x + 1]
        rows = [pair_rows(pair1, x, 4) for x in range(4)]
        sums = jnp.concatenate([q for r in rows for q in (r, r)], axis=0)
        out = jnp.dot(0.125 * sums, pool1, precision=HI, preferred_element_type=F32)
        for x in range(4):
            w2[x] = out[8 * x : 8 * x + 8]

    even = lanes_of((8, 128)) % 2 == 0

    def coarsen2(ref, out):
        for x in range(8):
            pair2[x] = ref[2 * x] + ref[2 * x + 1]
        for x in range(8):
            s = 0.125 * pair_rows(pair2, x, 8)
            out[x] = s + jnp.where(even, pltpu.roll(s, 127, 1), pltpu.roll(s, 1, 1))

    coarsen0(lambda x: kf[x + 4, 0:16, 0:128], wk)
    coarsen1(wk, 0)
    pack2(w2, sbk2)

    cell, rate = cell_ref[...], rate_ref[...]
    ix, iy, iz = cell // (64 * 512), cell // 512 % 64, cell % 512
    theirs = (ix // 16 * 4 + iy // 16) * 4 + iz // 128
    place = lax.rem(theirs - lax.rem(me + ROTATE, N) + 2 * N + 21, N)
    dx, dy, dz = place // 16, place // 4 % 4, place % 4
    fx, fy, fz = ix % 16 + 16 * (dx - 1) + 4, iy % 16 + 16 * (dy - 1), iz % 128 + 128 * (dz - 1)
    held = (dx < 3) & (dy < 3) & (dz < 3) & (fy >= -4) & (fy < 20) & (fz >= -4) & (fz < 132)
    fy, fz = jnp.where(fy < 0, fy + 24, fy), jnp.where(fz < 0, fz + 256, fz)
    rate = jnp.where(held, rate, 0.0)
    in_y = jnp.where(rows_of((24, 16)) == fy, rate, 0.0)
    in_z = jnp.where(rows_of((256, 16)) == fz, 1.0, 0.0)
    left = jnp.concatenate([jnp.where(fx == x, in_y, 0.0) for x in range(24)], axis=0)
    c0[...] = lax.dot_general(
        left, in_z, (((1,), (1,)), ((), ())), precision=HI, preferred_element_type=F32
    ).reshape(24, 24, 256)

    wait_got(rb2, recv.at[0])
    unpack0(0, 2, PLAN2, rb2, fr)
    unpack0(1, 2, PLAN2, rb2, kf)

    def coefs0(x):
        k, near = shifts0(kf, x)
        gs, total = coefs_of(k, near)
        for i in range(6):
            g0[i, x] = gs[i]
        t0[x] = (1.0 / OMEGA) * total
        c0[x] = OMEGA * c0[x] / total

    layer_loop(2, 22, coefs0)
    sweep0(fr, vb, g0, c0, 2, 22)
    sweep0(vb, u0, g0, c0, 3, 21)
    coarsen0(lambda x: own_residual0(u0, g0, c0, t0, x + 4)[1], w1)
    pack1([w1, wk], sbb1)
    send_plan(me, PLANS1[2][0], sbb1, rbb1, send.at[1], recv.at[1])
    for o in GATHER:
        start_to(me, sbk2, rbk2.at[SLOT[o]], send.at[2], recv.at[2], o)
    pack0(lambda a, x: u0[x + 4, 0:16, 0:128], 1, sbv)
    wait_sent(rb2, send.at[0])

    wait_got(rbb1, recv.at[1])
    unpack1(1, 2, wk, rbb1, k1)
    unpack1(0, 2, w1, rbb1, b1)

    def coefs1(x):
        k, near = shifts1(k1, x)
        gs, total = coefs_of(k, near)
        for i in range(6):
            g1[i, x] = gs[i]
        t1[x] = 0.25 * total
        c1[x] = OMEGA * b1[x] / t1[x]

    layer_loop(1, 15, coefs1)

    def sweep1(cur, out, low, high):
        def body(x):
            v, near = shifts1(cur, x)
            out[x] = v + change(v, near, [g1[i, x] for i in range(6)], c1[x])

        layer_loop(low, high, body)

    sweep1(c1, v1, 3, 13)

    def down1(x):
        v, near = shifts1(v1, x)
        r = change(v, near, [g1[i, x] for i in range(6)], c1[x]) * t1[x]
        q1[x] = (1.0 / OMEGA) * r[0:8]

    layer_loop(4, 12, down1)
    coarsen1(q1, 4)
    pack2(w2, sbb2)
    for o in GATHER:
        start_to(me, sbb2, rbb2.at[SLOT[o]], send.at[3], recv.at[3], o)
    half = lanes_of((8, 128)) < 64
    for x in range(8):
        v = v1[x + 4, 0:8]
        w1[x] = jnp.where(half, v, pltpu.roll(v, 64, 1))
    pack1([w1], sbv1)
    send_plan(me, PLANS1[1][0], sbv1, rbv1, send.at[4], recv.at[4])
    send_plan(me, PLANV, sbv, rbv, send.at[5], recv.at[5])

    rbk2[SLOT[0]] = sbk2[...]
    wait_got(rbk2.at[pl.ds(0, len(GATHER))], recv.at[2])
    unpack2(rbk2, k2)
    outside = lanes_of((16, 128)) // 32 == 2

    def fill2(x):
        k2[x] = jnp.where(outside, 1.0, k2[x])

    layer_loop(0, 16, fill2)

    def coefs2(x):
        k, near = shifts_round(k2, x, 4, 1)
        gs, total = coefs_of(k, near)
        for i in range(6):
            g2[i, x] = gs[i]
        t2[x] = 0.0625 * total

    layer_loop(0, 16, coefs2)
    coarsen2(k2, k3)

    def coefs3(x):
        k, near = shifts_round(k3, x, 2, 2)
        gs, total = coefs_of(k, near)
        for i in range(6):
            g3[i, x] = gs[i]
        t3[x] = 0.015625 * total

    layer_loop(0, 8, coefs3)

    wait_sent(rbb1, send.at[1])
    wait_sent(rbk2.at[pl.ds(0, len(GATHER))], send.at[2])

    rbb2[SLOT[0]] = sbb2[...]
    wait_got(rbb2.at[pl.ds(0, len(GATHER))], recv.at[3])
    unpack2(rbb2, b2)

    def first2(x):
        c2[x] = OMEGA * jnp.where(outside, 0.0, b2[x]) / t2[x]

    layer_loop(0, 16, first2)

    def sweep2(cur, out):
        def body(x):
            v, near = shifts_round(cur, x, 4, 1)
            out[x] = v + change(v, near, [g2[i, x] for i in range(6)], c2[x])

        layer_loop(0, 16, body)

    sweep2(c2, v2)

    def down2(x):
        v, near = shifts_round(v2, x, 4, 1)
        r = change(v, near, [g2[i, x] for i in range(6)], c2[x]) * t2[x]
        q2[x] = (1.0 / OMEGA) * r

    layer_loop(0, 16, down2)
    coarsen2(q2, c3)

    def first3(x):
        c3[x] = OMEGA * c3[x] / t3[x]

    layer_loop(0, 8, first3)

    def sweep3(cur, out):
        def body(x):
            v, near = shifts_round(cur, x, 2, 2)
            out[x] = v + change(v, near, [g3[i, x] for i in range(6)], c3[x])

        layer_loop(0, 8, body)

    sweep3(c3, v3)
    sweep3(v3, q3)
    sweep3(q3, v3)
    sweep3(v3, q3)
    sweep3(q3, v3)

    def up2(x):
        e = v3[x]
        exp3[x, pl.ds(0, 8, stride=2), :] = e
        exp3[x, pl.ds(1, 8, stride=2), :] = e
        q2[2 * x] = v2[2 * x] + exp3[x]
        q2[2 * x + 1] = v2[2 * x + 1] + exp3[x]

    layer_loop(0, 8, up2)
    sweep2(q2, v2)
    sweep2(v2, q2)

    wait_got(rbv1, recv.at[4])
    unpack1(0, 1, w1, rbv1, v1)
    spread2 = same((128, 128), lambda c, f: c == jnp.where(f < 96, f // 2, 64 + f // 2))
    row = rows_of((8, 128))
    order = [14, 15, 0, 1, 2, 3, 4, 5]
    rows = [jnp.where(row < 6, q2[x, 0:8], q2[(x - 4) % 16, 8:16]) for x in order]
    out = jnp.dot(jnp.concatenate(rows, axis=0), spread2, precision=HI, preferred_element_type=F32)
    for i in range(8):
        e = out[8 * i : 8 * i + 8]
        exp2[i, pl.ds(0, 8, stride=2), :] = e
        exp2[i, pl.ds(1, 8, stride=2), :] = e
    for x in range(16):
        b1[x] = v1[x] + exp2[x // 2]
    sweep1(b1, v1, 1, 15)
    sweep1(v1, b1, 2, 14)

    wait_got(rbv, recv.at[5])
    unpack0(0, 1, PLANV, rbv, u0)
    def spread(c, f):
        return c == jnp.where(f < 192, f // 2, f // 2)

    spread1 = same((128, 256), spread)
    inside = (lanes_of((16, 128)) < 66) | (lanes_of((16, 128)) >= 126)
    rows = [jnp.where(inside, b1[x], 0.0) for x in range(2, 14)]
    out = jnp.dot(jnp.concatenate(rows, axis=0), spread1, precision=HI, preferred_element_type=F32)
    low4 = rows_of((8, 256)) < 4
    for i in range(12):
        for h in range(2):
            e = out[16 * i : 16 * i + 16, 128 * h : 128 * h + 128]
            exp1[i, h, pl.ds(0, 16, stride=2), :] = e
            exp1[i, h, pl.ds(1, 16, stride=2), :] = e
    low4 = rows_of((8, 128)) < 4
    for i in range(12):
        for h in range(2):
            tail = jnp.where(low4, exp1[i, h, 16:24], exp1[i, h, 24:32])
            for x in (2 * i, 2 * i + 1):
                if 1 <= x < 23:
                    at = pl.ds(128 * h, 128)
                    vb[x, 0:16, at] = u0[x, 0:16, at] + exp1[i, h, 0:16]
                    vb[x, 16:24, at] = u0[x, 16:24, at] + tail
    sweep0(vb, u0, g0, c0, 2, 22)
    sweep0(u0, vb, g0, c0, 3, 21)

    def finish(x):
        v, r = own_residual0(vb, g0, c0, t0, x + 4)
        p_ref[0, x] = v[0:16, 0:128]
        r_ref[0, x] = r

    layer_loop(0, 16, finish)
    wait_sent(rbv1, send.at[4])
    wait_sent(rbv, send.at[5])
    wait_sent(rbb2.at[pl.ds(0, len(GATHER))], send.at[3])


def shards(perm_class, class_values, well_cells, well_rates, guess):
    wells = well_cells.shape[0]

    def f(*shape):
        return pltpu.VMEM(shape, F32)

    t = (8, 128)
    l0, l1, l2, l3 = (24, 24, 256), (16, 16, 128), (16, 16, 128), (8, 8, 128)
    vmem = pl.BlockSpec(memory_space=pltpu.VMEM)
    block = jax.ShapeDtypeStruct(guess.shape, F32)
    return pl.pallas_call(
        kernel,
        out_shape=(block, block),
        in_specs=[pl.BlockSpec(memory_space=pltpu.HBM)] * 5,
        out_specs=(vmem, vmem),
        scratch_shapes=[
            pltpu.VMEM(guess.shape[1:], jnp.int32), f(1, 8), pltpu.VMEM((1, wells), jnp.int32), f(1, wells), f(*l0), f(*l0), f(*l0), f(6, *l0), f(*l0), f(*l0), f(*l0),
            f(SEND2, *t), f(GOT2, *t), f(SENDV, *t), f(GOTV, *t),
            f(8, 16, 128), f(8, *t), f(8, *t), f(*l1), f(*l1), f(*l1), f(16, *t), f(6, *l1), f(*l1), f(*l1),
            *[f(n, *t) for narr in (2, 1) for n in PLANS1[narr][1:]],
            f(4, *t), f(4, *t), f(*l2), f(*l2), f(*l2), f(*l2), f(6, *l2), f(*l2), f(*l2),
            f(4, 128), f(len(GATHER) + 1, 4, 128), f(4, 128), f(len(GATHER) + 1, 4, 128),
            f(8, 16, 128), f(*l3), f(*l3), f(*l3), f(6, *l3), f(*l3), f(*l3),
            f(8, 16, 128), f(8, 16, 128), f(12, 2, 32, 128),
            pltpu.SemaphoreType.DMA((6,)), pltpu.SemaphoreType.DMA((6,)), pltpu.SemaphoreType.DMA((5,)),
        ],
        compiler_params=pltpu.CompilerParams(
            collective_id=0, has_side_effects=True, vmem_limit_bytes=40 * 1024 * 1024
        ),
    )(*[pltpu.with_memory_space_constraint(q, pltpu.HBM) for q in (perm_class, class_values.reshape(1, 8), well_cells.reshape(1, wells), well_rates.reshape(1, wells), guess)])


def solution(mesh):
    whole = P(("real", "space"), None, None, None)
    return jax.shard_map(
        shards,
        mesh=mesh,
        in_specs=(P("space", None, None, None), P(), P("real"), P("real"), whole),
        out_specs=(whole, whole),
        check_vma=False,
    )
```

```python
import functools

import jax
import jax.numpy as jnp
from jax import lax
from jax.experimental import pallas as pl
from jax.experimental.pallas import tpu as pltpu
from jax.sharding import PartitionSpec as P

N = 64
ROTATE = 21
OMEGA = 0.8
F32 = jnp.float32
HI = lax.Precision.HIGHEST
DIRS = [(a, b, c) for a in (-1, 0, 1) for b in (-1, 0, 1) for c in (-1, 0, 1) if (a, b, c) != (0, 0, 0)]


def offset(d):
    return (16 * d[0] + 4 * d[1] + d[2]) % N


def hops(off):
    total = 0
    for row in range(N):
        to = (row + off) % N
        y, z = abs(row // 16 - to // 16), abs(row // 2 % 8 - to // 2 % 8)
        total += min(y, 4 - y) + min(z, 8 - z) + 2 * abs(row % 2 - to % 2)
    return total


def sent0(narr):
    x_at = {1: 0, -1: 6 * narr}
    y_at = {1: 12 * narr, -1: 20 * narr}
    e_at = {d: 28 * narr + i for i, d in enumerate([(1, 1), (1, -1), (-1, 1), (-1, -1)])}
    z_at = {1: 28 * narr + 4, -1: 29 * narr + 4}
    return x_at, y_at, e_at, z_at, 30 * narr + 4


def plan0(narr):
    x_at, y_at, e_at, z_at, length = sent0(narr)
    plan, got = {}, 0
    for d in DIRS:
        dx, dy, dz = d
        if dy and dz:
            continue
        if dz:
            src, count = z_at[dz], narr
        elif dx and dy:
            src, count = e_at[(dx, dy)], 1
        elif dy:
            src, count = y_at[dy], 8 * narr
        else:
            src, count = x_at[dx], 6 * narr
        plan[d] = (src, got, count)
        got += count
    return plan, length, got


def plan1():
    plan, got = {}, 0
    for d in DIRS:
        dx, dy, dz = d
        if dz:
            continue
        src, count = (1 if dx < 0 else 0, 3) if dx else (0, 4)
        plan[d] = (src, got, count)
        got += count
    return plan, 4, got


PLAN2, SEND2, GOT2 = plan0(2)
PLANV, SENDV, GOTV = plan0(1)
PLAN1, SEND1, GOT1 = plan1()
SIDE2 = {(dz, dy): i for i, (dz, dy) in enumerate([(1, 1), (1, -1), (-1, 1), (-1, -1)])}
EDGE0 = {d: (SIDE2[(d[2], d[1])], i, 1) for i, d in enumerate(d for d in DIRS if d[1] and d[2])}
ENDS1 = {d: ((1 - d[2]) // 2, i, 1) for i, d in enumerate(d for d in DIRS if d[2])}
NEAR = sorted((offset(d) for d in DIRS), key=lambda o: (-hops(o), o))
GATHER = sorted((o for o in range(1, N) if o % 4 != 2), key=lambda o: (-hops(o), o))
SLOT = {o: i for i, o in enumerate(GATHER)}
SLOT[0] = len(GATHER)


def plan2():
    places, got = {}, 0
    for o in GATHER + [0]:
        side = {0: 0, 1: 1, 3: -1}[o % 4]
        places[o] = (0, got, 2) if side == 0 else (2 if side > 0 else 3, got, 1)
        got += places[o][2]
    return places, got


PART2, PARTS = plan2()


def rows_of(shape):
    return lax.broadcasted_iota(jnp.int32, shape, len(shape) - 2)


def lanes_of(shape):
    return lax.broadcasted_iota(jnp.int32, shape, len(shape) - 1)


def rot(v, by, axis):
    by %= v.shape[axis]
    return pltpu.roll(v, by, axis) if by else v


def layer_loop(low, high, body, unroll=None):
    def step(x, carry):
        body(x)
        return carry

    lax.fori_loop(low, high, step, 0, unroll=unroll or high - low)


def start_to(me, src, dst, send, recv, off):
    pltpu.make_async_remote_copy(
        src_ref=src,
        dst_ref=dst,
        send_sem=send,
        recv_sem=recv,
        device_id={"space": lax.rem(me + (N - off) % N, N)},
        device_id_type=pl.DeviceIdType.MESH,
    ).start()


def send_plan(me, plan, small, sb, rb, se, re, send, recv, i):
    for d in sorted(DIRS, key=lambda d: -hops(offset(d))):
        for messages, src, dst, sem in ((plan, sb, rb, i), (small, se, re, i + 1)):
            if d in messages:
                first, got, count = messages[d]
                start_to(
                    me, src.at[pl.ds(first, count)], dst.at[pl.ds(got, count)], send.at[sem], recv.at[sem], offset(d)
                )


def wait_got(rb, recv):
    pltpu.make_async_copy(rb, rb, recv).wait()


def wait_sent(rb, send):
    pltpu.make_async_copy(rb, rb, send).wait()


def pack0(own, narr, sb, se):
    x_at, y_at, e_at, z_at, _ = sent0(narr)
    low4 = rows_of((8, 128)) < 4
    two = rows_of((8, 128)) // 2
    group = lanes_of((16, 128)) // 4
    zlo = zhi = jnp.zeros((16, 128), F32)
    for a in range(narr):
        for i in range(3):
            for side, x in ((1, i), (-1, 13 + i)):
                v = own(a, x)
                sb[x_at[side] + a * 6 + 2 * i] = v[0:8]
                sb[x_at[side] + a * 6 + 2 * i + 1] = v[8:16]
        for i in range(8):
            v, w = own(a, i), own(a, i + 8)
            sb[y_at[1] + i * narr + a] = jnp.where(low4, v[0:8], rot(w[0:8], 4, 0))
            sb[y_at[-1] + i * narr + a] = jnp.where(low4, rot(w[8:16], 4, 0), v[8:16])
    for (dx, dy), at in e_at.items():
        z = jnp.zeros((8, 128), F32)
        for a in range(narr):
            for i in range(2):
                v = own(a, i if dx > 0 else 14 + i)
                v = v[0:8] if dy > 0 else v[8:16]
                z = jnp.where(two == 2 * a + i, rot(v, 4 * a + 2 * i - (0 if dy > 0 else 6), 0), z)
        sb[at] = z
    for a in range(narr):
        for x in range(16):
            v, g = own(a, x), 16 * a + x
            zlo = jnp.where(group == g, rot(v, 4 * g, 1), zlo)
            zhi = jnp.where(group == g, rot(v, 4 * g + 4, 1), zhi)
    for side, z in ((1, zlo), (-1, zhi)):
        if narr == 2:
            sb[z_at[side]] = z[0:8]
            sb[z_at[side] + 1] = z[8:16]
        else:
            sb[z_at[side]] = jnp.where(lanes_of((8, 128)) < 64, z[0:8], rot(z[8:16], 64, 1))
        se[SIDE2[(side, 1)]] = z[0:2]
        se[SIDE2[(side, -1)]] = z[14:16]


def unpack0(a, narr, plan, rb, re, out):
    low4 = rows_of((8, 128)) < 4

    def at(d):
        return plan[d][1]

    for i in range(3):
        for dx, base in ((1, 20), (-1, 1)):
            first = at((dx, 0, 0)) + a * 6 + 2 * i
            out[base + i, 0:8, 0:128] = rb[first]
            out[base + i, 8:16, 0:128] = rb[first + 1]
    for i in range(8):
        up, lo = rb[at((0, 1, 0)) + i * narr + a], rb[at((0, -1, 0)) + i * narr + a]
        out[4 + i, 16:24, 0:128] = jnp.where(low4, up, lo)
        out[12 + i, 16:24, 0:128] = rot(jnp.where(low4, lo, up), 4, 0)
    for dx, base in ((1, 20), (-1, 2)):
        for i in range(2):
            up = rot(rb[at((dx, 1, 0))], -(4 * a + 2 * i), 0)
            lo = rot(rb[at((dx, -1, 0))], 6 - (4 * a + 2 * i), 0)
            out[base + i, 16:24, 0:128] = jnp.where(low4, up, lo)
    half = lanes_of((24, 128)) < 64
    for dx, layers in ((0, range(4, 20)), (1, range(20, 23)), (-1, range(1, 4))):
        parts = {}
        for dz in (1, -1):
            mid = at((dx, 0, dz))
            up, lo = re[EDGE0[(dx, 1, dz)][1]], re[EDGE0[(dx, -1, dz)][1]]
            last = rb[mid + 1] if narr == 2 else rot(rb[mid], 64, 1)
            parts[dz] = jnp.concatenate([rb[mid], last, up, up, lo, lo], axis=0)
        for x in layers:
            g = 16 * a + (x - 4) % 16
            out[x, :, 128:256] = jnp.where(half, rot(parts[1], -4 * g, 1), rot(parts[-1], 124 - 4 * g, 1))


def shifts0(ref, x):
    v = ref[x]
    return v, (
        ref[x - 1],
        ref[x + 1],
        pltpu.roll(v, 1, 0),
        pltpu.roll(v, 23, 0),
        pltpu.roll(v, 1, 1),
        pltpu.roll(v, 255, 1),
    )


def coefs_of(k, near):
    faces = [k + n for n in near]
    total = ((faces[0] + faces[1]) + (faces[2] + faces[3])) + (faces[4] + faces[5])
    inv = OMEGA / total
    return [f * inv for f in faces], 0.5 * total


def change(v, near, gs, c):
    t = [g * (n - v) for g, n in zip(gs, near)]
    return c + (((t[0] + t[1]) + (t[2] + t[3])) + (t[4] + t[5]))


def sweep0(cur, out, g, c, low, high):
    def body(x):
        v, near = shifts0(cur, x)
        out[x] = v + change(v, near, [g[i, x] for i in range(6)], c[x])

    layer_loop(low, high, body)


def own_residual0(cur, g, c, t, x):
    v, near = shifts0(cur, x)
    r = change(v, near, [g[i, x] for i in range(6)], c[x]) * t[x]
    return v, r[0:16, 0:128]


def pack1(w, sb, se):
    half, group = lanes_of((8, 128)) < 64, lanes_of((8, 128)) // 8
    for j in range(4):
        sb[j] = jnp.where(half, w[2 * j], w[2 * j + 1])
    for i in range(2):
        z = jnp.zeros((8, 128), F32)
        for x in range(8):
            z = jnp.where(group == x, rot(w[x], 8 * x - 56 * i, 1), z)
        se[i] = jnp.where(half, z, rot(rot(z, 4, 0), 64, 1))[0:4]


def unpack1(w, rb, re, out):
    half, quarter = lanes_of((8, 128)) < 64, lanes_of((8, 128)) < 96

    def block(dx, dy, x):
        if (dx, dy) == (0, 0):
            return w[x]
        tile = rb[PLAN1[(dx, dy, 0)][1] + x // 2 - (1 if dx < 0 else 0)]
        return rot(tile, 64, 1) if x % 2 else tile

    for dx, layers in ((0, range(8)), (1, range(6)), (-1, range(2, 8))):
        for t, dy in enumerate((0, 1, -1)):
            up, lo = re[ENDS1[(dx, dy, 1)][1]], re[ENDS1[(dx, dy, -1)][1]]
            up, lo = (jnp.concatenate([q, rot(q, 64, 1)], axis=0) for q in (up, lo))
            for x in layers:
                ends = jnp.where(quarter, rot(up, 64 - 8 * x, 1), rot(lo, 120 - 8 * x, 1))
                out[6 + x + 8 * dx, 8 * t : 8 * t + 8] = jnp.where(half, block(dx, dy, x), ends)


def shifts1(ref, x):
    v = ref[x]
    return v, (
        ref[x - 1],
        ref[x + 1],
        pltpu.roll(v, 1, 0),
        pltpu.roll(v, 23, 0),
        pltpu.roll(v, 1, 1),
        pltpu.roll(v, 127, 1),
    )


def shifts_round(ref, x, step, lane_step):
    layers, rows = ref.shape[0], ref.shape[1]
    v = ref[x]
    row = rows_of(v.shape)
    below, above = ref[lax.rem(x + layers - step, layers)], ref[lax.rem(x + step, layers)]
    return v, (
        ref[lax.rem(x + layers - 1, layers)],
        ref[lax.rem(x + 1, layers)],
        pltpu.roll(jnp.where(row == rows - 1, below, v), 1, 0),
        pltpu.roll(jnp.where(row == 0, above, v), rows - 1, 0),
        pltpu.roll(v, lane_step, 1),
        pltpu.roll(v, 128 - lane_step, 1),
    )


def pack2(w2, sb):
    group = lanes_of((8, 128)) // 32
    z = w2[0]
    for x in range(1, 4):
        z = jnp.where(group == x, w2[x], z)
    sb[...] = z[0:4]


def unpack2(rb, out):
    group = lanes_of((8, 128)) // 32
    for cx in range(4):
        for t in range(2):
            tiles = {}
            for dz in (-1, 0, 1):
                first = rb[SLOT[(16 * cx + 8 * t + dz) % N]]
                second = rb[SLOT[(16 * cx + 8 * t + 4 + dz) % N]]
                tiles[dz] = jnp.concatenate([first, second], axis=0)
            for x in range(4):
                z = rot(tiles[0], -32 * x, 1)
                z = jnp.where(group == 1, rot(tiles[1], 32 - 32 * x, 1), z)
                z = jnp.where(group == 3, rot(tiles[-1], 96 - 32 * x, 1), z)
                out[4 * cx + x, 8 * t : 8 * t + 8] = z


def pack_parts(main, ends, low, high, sb):
    lane = lanes_of((8, 128))
    inner = main[1]
    outer = jnp.where(lane < 32, main[0], main[5])
    up, lo = low[0], high[0]
    for x in range(1, 4):
        inner = jnp.where(lane // 32 == x, main[x + 1], inner)
    for x in range(1, 6):
        up = jnp.where(lane // 16 == x, low[x], up)
        lo = jnp.where(lane // 16 == x, high[x], lo)
    for x in range(6):
        outer = jnp.where((lane == 97 + 2 * x) | (lane == 112 + 2 * x), ends[x], outer)
        up = jnp.where(lane == 96 + 2 * x, ends[x], up)
        lo = jnp.where(lane == 113 + 2 * x, ends[x], lo)
    for i, tile in enumerate((inner, outer, up, lo)):
        sb[i] = tile


def sum_parts(rb, out):
    lane, row = lanes_of((8, 128)), rows_of((8, 128))
    odd = lane % 2 == 1

    def column(cx, cy):
        first = PART2[(16 * cx + 4 * cy) % N][1]
        inner, outer = rb[first], rb[first + 1]
        up = rb[PART2[(16 * cx + 4 * cy + 1) % N][1]]
        lo = rb[PART2[(16 * cx + 4 * cy - 1) % N][1]]
        above, below = jnp.where(odd, outer, up), jnp.where(odd, lo, outer)
        layers = []
        for x in range(6):
            own = rot(inner, -32 * (x - 1), 1) if 0 < x < 5 else rot(outer, -32 * (x // 5), 1)
            z = jnp.where(lane < 48, rot(up, 32 - 16 * x, 1), rot(lo, 112 - 16 * x, 1))
            z = jnp.where((lane >= 48) & (lane < 112), 0.0, z)
            z = jnp.where(lane < 32, own, z)
            e = jnp.where((lane == 31) | (lane == 32), rot(above, 31 - 96 - 2 * x, 1), 0.0)
            e = jnp.where((lane == 127) | (lane == 0), rot(below, 15 - 2 * x, 1), e)
            layers.append(z + e)
        return layers

    even = {(cx, t): column(cx, 2 * t) for cx in range(4) for t in range(2)}
    turned = {
        (cx, t): [pltpu.roll(q, 4, 0) for q in column(cx, 2 * t + 1)] for cx in range(4) for t in range(2)
    }
    rows = {}
    for cx in range(4):
        for t in range(2):
            after = even[(cx, 1) if t == 0 else ((cx + 1) % 4, 0)]
            before = turned[(cx, 0) if t == 1 else ((cx - 1) % 4, 1)]
            rows[(cx, t)] = [
                jnp.where(row < 5, even[(cx, t)][x], after[x]) + jnp.where(row >= 3, turned[(cx, t)][x], before[x])
                for x in range(6)
            ]
    for cx in range(4):
        for t in range(2):
            for x in range(4):
                z = rows[(cx, t)][x + 1]
                if x == 0:
                    z = z + rows[((cx - 1) % 4, t)][5]
                if x == 3:
                    z = z + rows[((cx + 1) % 4, t)][0]
                out[4 * cx + x, 8 * t : 8 * t + 8] = z


def pair_rows(ref, index, count):
    return ref[index, pl.ds(0, count, stride=2), :] + ref[index, pl.ds(1, count, stride=2), :]


def kernel(
    cls_hbm, val_hbm, cell_hbm, rate_hbm, guess_hbm, p_ref, r_ref,
    cls_ref, val_ref, cell_ref, rate_ref, fr, vb, kf, g0, t0, c0, u0, sb2, rb2, sbv, rbv, se2, re2, sev, rev,
    pair, w1, wk, k1, b1, v1, g1, t1, c1, sbk1, rbk1, sbb1, rbb1, sek1, rek1, seb1, reb1,
    pair1, part, w2, k2, b2, v2, q2, g2, t2, c2, sbk2, rbk2, sbb2, rbb2,
    pair2, k3, v3, q3, g3, t3, c3, exp3, exp2, exp1, send, recv, load,
):
    me = lax.axis_index("space")
    loads = [
        pltpu.make_async_copy(src, dst, load.at[i])
        for i, (src, dst) in enumerate(
            [
                (cls_hbm.at[0], cls_ref),
                (val_hbm, val_ref),
                (guess_hbm.at[0], fr.at[pl.ds(4, 16), pl.ds(0, 16), pl.ds(0, 128)]),
                (cell_hbm, cell_ref),
                (rate_hbm, rate_ref),
            ]
        )
    ]
    for copy in loads:
        copy.start()
    barrier = pltpu.get_barrier_semaphore()
    for o in GATHER:
        pl.semaphore_signal(
            barrier, inc=1, device_id={"space": lax.rem(me + o, N)}, device_id_type=pl.DeviceIdType.MESH
        )

    for copy in loads:
        copy.wait()
    vals = [jnp.broadcast_to(val_ref[0:1, i : i + 1], (16, 128)) for i in range(8)]

    def lookup(x):
        cls = cls_ref[x]
        bits = [(cls & 1) == 0, (cls & 2) == 0, (cls & 4) == 0]
        pairs = [jnp.where(bits[0], vals[2 * i], vals[2 * i + 1]) for i in range(4)]
        quads = [jnp.where(bits[1], pairs[0], pairs[1]), jnp.where(bits[1], pairs[2], pairs[3])]
        kf[x + 4, 0:16, 0:128] = jnp.where(bits[2], quads[0], quads[1])

    layer_loop(0, 16, lookup)
    pack0(lambda a, x: (fr if a == 0 else kf)[x + 4, 0:16, 0:128], 2, sb2, se2)
    pl.semaphore_wait(barrier, len(GATHER))
    send_plan(me, PLAN2, EDGE0, sb2, rb2, se2, re2, send, recv, 0)

    def same(shape, f):
        return f(rows_of(shape), lanes_of(shape)).astype(F32)

    pool0 = same((128, 128), lambda l, c: l // 2 == c % 64)
    pool1 = same((128, 128), lambda l, c: (l // 2 == c % 32) & (l < 64))

    def coarsen0(layer, w1):
        def body(x):
            pair[x] = layer(2 * x) + layer(2 * x + 1)

        layer_loop(0, 8, body)
        sums = jnp.concatenate([pair_rows(pair, x, 8) for x in range(8)], axis=0)
        out = jnp.dot(0.125 * sums, pool0, precision=HI, preferred_element_type=F32)
        for x in range(8):
            w1[x] = out[8 * x : 8 * x + 8]

    def coarsen1(ref, base):
        for x in range(4):
            pair1[x] = ref[base + 2 * x] + ref[base + 2 * x + 1]
        rows = [pair_rows(pair1, x, 4) for x in range(4)]
        sums = jnp.concatenate([q for r in rows for q in (r, r)], axis=0)
        out = jnp.dot(0.125 * sums, pool1, precision=HI, preferred_element_type=F32)
        for x in range(4):
            w2[x] = out[8 * x : 8 * x + 8]

    even = lanes_of((8, 128)) % 2 == 0

    def pool_parts(l, c):
        z = jnp.where(l < 64, l // 2, jnp.where(l < 66, 32, jnp.where(l >= 126, -1, -2)))
        main, ends = z == c % 32, z == jnp.where(c % 2 == 0, -1, 32)
        low, high = z == c % 16, z == 16 + c % 16
        return ((c < 128) & main) | ((c // 128 == 1) & ends) | ((c // 128 == 2) & low) | ((c // 128 == 3) & high)

    def coarsen2(ref, out):
        for x in range(8):
            pair2[x] = ref[2 * x] + ref[2 * x + 1]
        for x in range(8):
            s = 0.125 * pair_rows(pair2, x, 8)
            out[x] = s + jnp.where(even, pltpu.roll(s, 127, 1), pltpu.roll(s, 1, 1))

    coarsen0(lambda x: kf[x + 4, 0:16, 0:128], wk)
    pack1(wk, sbk1, sek1)
    send_plan(me, PLAN1, ENDS1, sbk1, rbk1, sek1, rek1, send, recv, 2)
    coarsen1(wk, 0)
    pack2(w2, sbk2)
    for o in GATHER:
        start_to(me, sbk2, rbk2.at[SLOT[o]], send.at[8], recv.at[8], o)

    cell, rate = cell_ref[...], rate_ref[...]
    ix, iy, iz = cell // (64 * 512), cell // 512 % 64, cell % 512
    theirs = (ix // 16 * 4 + iy // 16) * 4 + iz // 128
    place = lax.rem(theirs - lax.rem(me + ROTATE, N) + 2 * N + 21, N)
    dx, dy, dz = place // 16, place // 4 % 4, place % 4
    fx, fy, fz = ix % 16 + 16 * (dx - 1) + 4, iy % 16 + 16 * (dy - 1), iz % 128 + 128 * (dz - 1)
    held = (dx < 3) & (dy < 3) & (dz < 3) & (fy >= -4) & (fy < 20) & (fz >= -4) & (fz < 132)
    fy, fz = jnp.where(fy < 0, fy + 24, fy), jnp.where(fz < 0, fz + 256, fz)
    rate = jnp.where(held, rate, 0.0)
    in_y = jnp.where(rows_of((24, 16)) == fy, rate, 0.0)
    in_z = jnp.where(rows_of((256, 16)) == fz, 1.0, 0.0)
    left = jnp.concatenate([jnp.where(fx == x, in_y, 0.0) for x in range(24)], axis=0)
    c0[...] = lax.dot_general(
        left, in_z, (((1,), (1,)), ((), ())), precision=HI, preferred_element_type=F32
    ).reshape(24, 24, 256)

    wait_got(rb2, recv.at[0])
    wait_got(re2, recv.at[1])
    unpack0(0, 2, PLAN2, rb2, re2, fr)
    unpack0(1, 2, PLAN2, rb2, re2, kf)

    def coefs0(x):
        k, near = shifts0(kf, x)
        gs, total = coefs_of(k, near)
        for i in range(6):
            g0[i, x] = gs[i]
        t0[x] = (1.0 / OMEGA) * total
        c0[x] = OMEGA * c0[x] / total

    layer_loop(2, 22, coefs0)
    sweep0(fr, vb, g0, c0, 2, 22)
    sweep0(vb, u0, g0, c0, 3, 21)
    coarsen0(lambda x: own_residual0(u0, g0, c0, t0, x + 4)[1], w1)

    own1 = lanes_of((8, 128)) < 64

    def part1(x):
        b1[x] = jnp.zeros((24, 128), F32)
        v1[x] = jnp.zeros((24, 128), F32)

    layer_loop(3, 17, part1)
    wait_got(rbk1, recv.at[2])
    wait_got(rek1, recv.at[3])
    unpack1(wk, rbk1, rek1, k1)

    def coefs1(x):
        k, near = shifts1(k1, x)
        gs, total = coefs_of(k, near)
        for i in range(6):
            g1[i, x] = gs[i]
        t1[x] = 0.25 * total

    layer_loop(1, 19, coefs1)
    for x in range(8):
        b1[6 + x, 0:8] = jnp.where(own1, OMEGA * w1[x] / t1[6 + x, 0:8], 0.0)

    def sweep1(cur, out, c, low, high):
        def body(x):
            v, near = shifts1(cur, x)
            out[x] = v + change(v, near, [g1[i, x] for i in range(6)], c[x])

        layer_loop(low, high, body)

    sweep1(b1, v1, b1, 5, 15)
    low4 = rows_of((8, 128)) < 4

    def down1(x):
        v, near = shifts1(v1, x)
        return change(v, near, [g1[i, x] for i in range(6)], b1[x]) * t1[x]

    for i in range(6):
        q = down1(4 + 2 * i) + down1(5 + 2 * i)
        part[i, 0:8] = q[0:8]
        part[i, 8:16] = jnp.where(low4, q[8:16], q[16:24])
    sums = jnp.concatenate([pair_rows(part, x, 8) for x in range(6)], axis=0)
    wide = same((128, 512), pool_parts)
    out = jnp.dot((0.125 / OMEGA) * sums, wide, precision=HI, preferred_element_type=F32)
    pieces = [[out[8 * x : 8 * x + 8, 128 * i : 128 * i + 128] for x in range(6)] for i in range(4)]
    pack_parts(*pieces, sbb2)

    def gather(offsets):
        for o in offsets:
            src, got, count = PART2[o]
            start_to(me, sbb2.at[pl.ds(src, count)], rbb2.at[pl.ds(got, count)], send.at[9], recv.at[9], o)

    gather(GATHER[:24])
    pack1(w1, sbb1, seb1)
    send_plan(me, PLAN1, ENDS1, sbb1, rbb1, seb1, reb1, send, recv, 4)
    gather(GATHER[24:])
    pack0(lambda a, x: u0[x + 4, 0:16, 0:128], 1, sbv, sev)
    send_plan(me, PLANV, EDGE0, sbv, rbv, sev, rev, send, recv, 6)
    for i, buffer in enumerate((rb2, re2, rbk1, rek1)):
        wait_sent(buffer, send.at[i])

    rbk2[SLOT[0]] = sbk2[...]
    wait_got(rbk2.at[pl.ds(0, len(GATHER))], recv.at[8])
    unpack2(rbk2, k2)
    outside = lanes_of((16, 128)) // 32 == 2

    def fill2(x):
        k2[x] = jnp.where(outside, 1.0, k2[x])

    layer_loop(0, 16, fill2)

    def coefs2(x):
        k, near = shifts_round(k2, x, 4, 1)
        gs, total = coefs_of(k, near)
        for i in range(6):
            g2[i, x] = gs[i]
        t2[x] = 0.0625 * total

    layer_loop(0, 16, coefs2)
    coarsen2(k2, k3)

    def coefs3(x):
        k, near = shifts_round(k3, x, 2, 2)
        gs, total = coefs_of(k, near)
        for i in range(6):
            g3[i, x] = gs[i]
        t3[x] = 0.015625 * total

    layer_loop(0, 8, coefs3)

    wait_sent(rbk2.at[pl.ds(0, len(GATHER))], send.at[8])

    wait_got(rbb1, recv.at[4])
    wait_got(reb1, recv.at[5])
    unpack1(w1, rbb1, reb1, b1)

    def first1(x):
        c1[x] = OMEGA * b1[x] / t1[x]

    layer_loop(1, 19, first1)
    sweep1(c1, v1, c1, 2, 18)
    wait_sent(rbb1, send.at[4])
    wait_sent(reb1, send.at[5])

    for i in range(2):
        rbb2[PARTS - 2 + i] = sbb2[i]
    wait_got(rbb2.at[pl.ds(0, PARTS - 2)], recv.at[9])
    sum_parts(rbb2, b2)

    def first2(x):
        c2[x] = OMEGA * jnp.where(outside, 0.0, b2[x]) / t2[x]

    layer_loop(0, 16, first2)

    def sweep2(cur, out):
        def body(x):
            v, near = shifts_round(cur, x, 4, 1)
            out[x] = v + change(v, near, [g2[i, x] for i in range(6)], c2[x])

        layer_loop(0, 16, body)

    sweep2(c2, v2)

    def down2(x):
        v, near = shifts_round(v2, x, 4, 1)
        r = change(v, near, [g2[i, x] for i in range(6)], c2[x]) * t2[x]
        q2[x] = (1.0 / OMEGA) * r

    layer_loop(0, 16, down2)
    coarsen2(q2, c3)

    def first3(x):
        c3[x] = OMEGA * c3[x] / t3[x]

    layer_loop(0, 8, first3)

    def sweep3(cur, out):
        def body(x):
            v, near = shifts_round(cur, x, 2, 2)
            out[x] = v + change(v, near, [g3[i, x] for i in range(6)], c3[x])

        layer_loop(0, 8, body)

    sweep3(c3, v3)
    sweep3(v3, q3)
    sweep3(q3, v3)
    sweep3(v3, q3)
    sweep3(q3, v3)

    def up2(x):
        e = v3[x]
        exp3[x, pl.ds(0, 8, stride=2), :] = e
        exp3[x, pl.ds(1, 8, stride=2), :] = e
        q2[2 * x] = v2[2 * x] + exp3[x]
        q2[2 * x + 1] = v2[2 * x + 1] + exp3[x]

    layer_loop(0, 8, up2)
    sweep2(q2, v2)
    sweep2(v2, q2)

    spread2 = same((128, 128), lambda c, f: c == jnp.where(f < 96, f // 2, 64 + f // 2))
    row = rows_of((8, 128))
    order = [14, 15, 0, 1, 2, 3, 4, 5]
    rows = [jnp.where(row < 6, q2[x, 0:8], q2[(x - 4) % 16, 8:16]) for x in order]
    out = jnp.dot(jnp.concatenate(rows, axis=0), spread2, precision=HI, preferred_element_type=F32)
    for i in range(8):
        e = out[8 * i : 8 * i + 8]
        exp2[i, pl.ds(0, 8, stride=2), :] = e
        exp2[i, pl.ds(1, 8, stride=2), :] = e
    for x in range(2, 18):
        b1[x, 0:16] = v1[x, 0:16] + exp2[(x - 2) // 2]
        b1[x, 16:24] = v1[x, 16:24] + exp2[(x - 2) // 2, 8:16]
    sweep1(b1, v1, c1, 3, 17)
    sweep1(v1, b1, c1, 4, 16)

    wait_got(rbv, recv.at[6])
    wait_got(rev, recv.at[7])
    unpack0(0, 1, PLANV, rbv, rev, u0)
    spread1 = same((128, 256), lambda c, f: c == f // 2)
    rows = [q for x in range(4, 16) for q in (b1[x, 0:8], jnp.where(low4, b1[x, 8:16], b1[x, 16:24]))]
    out = jnp.dot(jnp.concatenate(rows, axis=0), spread1, precision=HI, preferred_element_type=F32)
    for i in range(12):
        for h in range(2):
            e = out[16 * i : 16 * i + 16, 128 * h : 128 * h + 128]
            exp1[i, h, pl.ds(0, 16, stride=2), :] = e
            exp1[i, h, pl.ds(1, 16, stride=2), :] = e
    for i in range(12):
        for h in range(2):
            tail = jnp.where(low4, exp1[i, h, 16:24], exp1[i, h, 24:32])
            for x in (2 * i, 2 * i + 1):
                if 1 <= x < 23:
                    at = pl.ds(128 * h, 128)
                    vb[x, 0:16, at] = u0[x, 0:16, at] + exp1[i, h, 0:16]
                    vb[x, 16:24, at] = u0[x, 16:24, at] + tail
    sweep0(vb, u0, g0, c0, 2, 22)
    sweep0(u0, vb, g0, c0, 3, 21)

    def finish(x):
        v, r = own_residual0(vb, g0, c0, t0, x + 4)
        p_ref[0, x] = v[0:16, 0:128]
        r_ref[0, x] = r

    layer_loop(0, 16, finish)
    wait_sent(rbv, send.at[6])
    wait_sent(rev, send.at[7])
    wait_sent(rbb2.at[pl.ds(0, PARTS - 2)], send.at[9])


def shards(perm_class, class_values, well_cells, well_rates, guess):
    wells = well_cells.shape[0]

    def f(*shape):
        return pltpu.VMEM(shape, F32)

    t = (8, 128)
    l0, l1, l2, l3 = (24, 24, 256), (20, 24, 128), (16, 16, 128), (8, 8, 128)
    vmem = pl.BlockSpec(memory_space=pltpu.VMEM)
    block = jax.ShapeDtypeStruct(guess.shape, F32)
    return pl.pallas_call(
        kernel,
        out_shape=(block, block),
        in_specs=[pl.BlockSpec(memory_space=pltpu.HBM)] * 5,
        out_specs=(vmem, vmem),
        scratch_shapes=[
            pltpu.VMEM(guess.shape[1:], jnp.int32), f(1, 8), pltpu.VMEM((1, wells), jnp.int32), f(1, wells), f(*l0), f(*l0), f(*l0), f(6, *l0), f(*l0), f(*l0), f(*l0),
            f(SEND2, *t), f(GOT2, *t), f(SENDV, *t), f(GOTV, *t), *([f(4, 2, 128), f(len(EDGE0), 2, 128)] * 2),
            f(8, 16, 128), f(8, *t), f(8, *t), f(*l1), f(*l1), f(*l1), f(6, *l1), f(*l1), f(*l1),
            *([f(SEND1, *t), f(GOT1, *t)] * 2), *([f(2, 4, 128), f(len(ENDS1), 4, 128)] * 2),
            f(4, *t), f(6, 16, 128), f(4, *t), f(*l2), f(*l2), f(*l2), f(*l2), f(6, *l2), f(*l2), f(*l2),
            f(4, 128), f(len(GATHER) + 1, 4, 128), f(4, *t), f(PARTS, *t),
            f(8, 16, 128), f(*l3), f(*l3), f(*l3), f(6, *l3), f(*l3), f(*l3),
            f(8, 16, 128), f(8, 16, 128), f(12, 2, 32, 128),
            pltpu.SemaphoreType.DMA((10,)), pltpu.SemaphoreType.DMA((10,)), pltpu.SemaphoreType.DMA((5,)),
        ],
        compiler_params=pltpu.CompilerParams(
            collective_id=0, has_side_effects=True, vmem_limit_bytes=40 * 1024 * 1024
        ),
    )(*[pltpu.with_memory_space_constraint(q, pltpu.HBM) for q in (perm_class, class_values.reshape(1, 8), well_cells.reshape(1, wells), well_rates.reshape(1, wells), guess)])


def solution(mesh):
    whole = P(("real", "space"), None, None, None)
    return jax.shard_map(
        shards,
        mesh=mesh,
        in_specs=(P("space", None, None, None), P(), P("real"), P("real"), whole),
        out_specs=(whole, whole),
        check_vma=False,
    )
```

```python
import functools

import jax
import jax.numpy as jnp
from jax import lax
from jax.experimental import pallas as pl
from jax.experimental.pallas import tpu as pltpu
from jax.sharding import PartitionSpec as P

N = 64
ROTATE = 21
OMEGA = 0.8
F32 = jnp.float32
HI = lax.Precision.HIGHEST
DIRS = [(a, b, c) for a in (-1, 0, 1) for b in (-1, 0, 1) for c in (-1, 0, 1) if (a, b, c) != (0, 0, 0)]


def offset(d):
    return (16 * d[0] + 4 * d[1] + d[2]) % N


def hops(off):
    total = 0
    for row in range(N):
        to = (row + off) % N
        y, z = abs(row // 16 - to // 16), abs(row // 2 % 8 - to // 2 % 8)
        total += min(y, 4 - y) + min(z, 8 - z) + 2 * abs(row % 2 - to % 2)
    return total


def sent0(narr):
    x_at = {1: 0, -1: 6 * narr}
    y_at = {1: 12 * narr, -1: 20 * narr}
    e_at = {d: 28 * narr + i for i, d in enumerate([(1, 1), (1, -1), (-1, 1), (-1, -1)])}
    z_at = {1: 28 * narr + 4, -1: 29 * narr + 4}
    return x_at, y_at, e_at, z_at, 30 * narr + 4


def plan0(narr):
    x_at, y_at, e_at, z_at, length = sent0(narr)
    plan, got = {}, 0
    for d in DIRS:
        dx, dy, dz = d
        if dy and dz:
            continue
        if dz:
            src, count = z_at[dz], narr
        elif dx and dy:
            src, count = e_at[(dx, dy)], 1
        elif dy:
            src, count = y_at[dy], 8 * narr
        else:
            src, count = x_at[dx], 6 * narr
        plan[d] = (src, got, count)
        got += count
    return plan, length, got


def plan1():
    plan, got = {}, 0
    for d in DIRS:
        dx, dy, dz = d
        if dz:
            continue
        src, count = (1 if dx < 0 else 0, 3) if dx else (0, 4)
        plan[d] = (src, got, count)
        got += count
    return plan, 4, got


PLAN2, SEND2, GOT2 = plan0(2)
PLANV, SENDV, GOTV = plan0(1)
PLAN1, SEND1, GOT1 = plan1()
SIDE2 = {(dz, dy): i for i, (dz, dy) in enumerate([(1, 1), (1, -1), (-1, 1), (-1, -1)])}
EDGE0 = {d: (SIDE2[(d[2], d[1])], i, 1) for i, d in enumerate(d for d in DIRS if d[1] and d[2])}
ENDS1 = {d: ((1 - d[2]) // 2, i, 1) for i, d in enumerate(d for d in DIRS if d[2])}
NEAR = sorted((offset(d) for d in DIRS), key=lambda o: (-hops(o), o))
GATHER = sorted((o for o in range(1, N) if o % 4 != 2), key=lambda o: (-hops(o), o))
SLOT = {o: i for i, o in enumerate(GATHER)}
SLOT[0] = len(GATHER)


def plan2():
    places, got = {}, 0
    for o in GATHER + [0]:
        side = {0: 0, 1: 1, 3: -1}[o % 4]
        places[o] = (0, got, 2) if side == 0 else (2 if side > 0 else 3, got, 1)
        got += places[o][2]
    return places, got


PART2, PARTS = plan2()


def rows_of(shape):
    return lax.broadcasted_iota(jnp.int32, shape, len(shape) - 2)


def lanes_of(shape):
    return lax.broadcasted_iota(jnp.int32, shape, len(shape) - 1)


def rot(v, by, axis):
    by %= v.shape[axis]
    return pltpu.roll(v, by, axis) if by else v


def layer_loop(low, high, body, unroll=None):
    def step(x, carry):
        body(x)
        return carry

    lax.fori_loop(low, high, step, 0, unroll=unroll or high - low)


def start_to(me, src, dst, send, recv, off):
    pltpu.make_async_remote_copy(
        src_ref=src,
        dst_ref=dst,
        send_sem=send,
        recv_sem=recv,
        device_id={"space": lax.rem(me + (N - off) % N, N)},
        device_id_type=pl.DeviceIdType.MESH,
    ).start()


def send_plan(me, plan, small, sb, rb, se, re, send, recv, i):
    for d in sorted(DIRS, key=lambda d: -hops(offset(d))):
        for messages, src, dst, sem in ((plan, sb, rb, i), (small, se, re, i + 1)):
            if d in messages:
                first, got, count = messages[d]
                start_to(
                    me, src.at[pl.ds(first, count)], dst.at[pl.ds(got, count)], send.at[sem], recv.at[sem], offset(d)
                )


def wait_got(rb, recv):
    pltpu.make_async_copy(rb, rb, recv).wait()


def wait_sent(rb, send):
    pltpu.make_async_copy(rb, rb, send).wait()


def pack0(own, narr, sb, se):
    x_at, y_at, e_at, z_at, _ = sent0(narr)
    low4 = rows_of((8, 128)) < 4
    two = rows_of((8, 128)) // 2
    group = lanes_of((16, 128)) // 4
    zlo = zhi = jnp.zeros((16, 128), F32)
    for a in range(narr):
        for i in range(3):
            for side, x in ((1, i), (-1, 13 + i)):
                v = own(a, x)
                sb[x_at[side] + a * 6 + 2 * i] = v[0:8]
                sb[x_at[side] + a * 6 + 2 * i + 1] = v[8:16]
        for i in range(8):
            v, w = own(a, i), own(a, i + 8)
            sb[y_at[1] + i * narr + a] = jnp.where(low4, v[0:8], rot(w[0:8], 4, 0))
            sb[y_at[-1] + i * narr + a] = jnp.where(low4, rot(w[8:16], 4, 0), v[8:16])
    for (dx, dy), at in e_at.items():
        z = jnp.zeros((8, 128), F32)
        for a in range(narr):
            for i in range(2):
                v = own(a, i if dx > 0 else 14 + i)
                v = v[0:8] if dy > 0 else v[8:16]
                z = jnp.where(two == 2 * a + i, rot(v, 4 * a + 2 * i - (0 if dy > 0 else 6), 0), z)
        sb[at] = z
    for a in range(narr):
        for x in range(16):
            v, g = own(a, x), 16 * a + x
            zlo = jnp.where(group == g, rot(v, 4 * g, 1), zlo)
            zhi = jnp.where(group == g, rot(v, 4 * g + 4, 1), zhi)
    for side, z in ((1, zlo), (-1, zhi)):
        if narr == 2:
            sb[z_at[side]] = z[0:8]
            sb[z_at[side] + 1] = z[8:16]
        else:
            sb[z_at[side]] = jnp.where(lanes_of((8, 128)) < 64, z[0:8], rot(z[8:16], 64, 1))
        se[SIDE2[(side, 1)]] = z[0:2]
        se[SIDE2[(side, -1)]] = z[14:16]


def unpack0(a, narr, plan, rb, re, out):
    low4 = rows_of((8, 128)) < 4

    def at(d):
        return plan[d][1]

    for i in range(3):
        for dx, base in ((1, 20), (-1, 1)):
            first = at((dx, 0, 0)) + a * 6 + 2 * i
            out[base + i, 0:8, 0:128] = rb[first]
            out[base + i, 8:16, 0:128] = rb[first + 1]
    for i in range(8):
        up, lo = rb[at((0, 1, 0)) + i * narr + a], rb[at((0, -1, 0)) + i * narr + a]
        out[4 + i, 16:24, 0:128] = jnp.where(low4, up, lo)
        out[12 + i, 16:24, 0:128] = rot(jnp.where(low4, lo, up), 4, 0)
    for dx, base in ((1, 20), (-1, 2)):
        for i in range(2):
            up = rot(rb[at((dx, 1, 0))], -(4 * a + 2 * i), 0)
            lo = rot(rb[at((dx, -1, 0))], 6 - (4 * a + 2 * i), 0)
            out[base + i, 16:24, 0:128] = jnp.where(low4, up, lo)
    half = lanes_of((24, 128)) < 64
    for dx, layers in ((0, range(4, 20)), (1, range(20, 23)), (-1, range(1, 4))):
        parts = {}
        for dz in (1, -1):
            mid = at((dx, 0, dz))
            up, lo = re[EDGE0[(dx, 1, dz)][1]], re[EDGE0[(dx, -1, dz)][1]]
            last = rb[mid + 1] if narr == 2 else rot(rb[mid], 64, 1)
            parts[dz] = jnp.concatenate([rb[mid], last, up, up, lo, lo], axis=0)
        for x in layers:
            g = 16 * a + (x - 4) % 16
            out[x, :, 128:256] = jnp.where(half, rot(parts[1], -4 * g, 1), rot(parts[-1], 124 - 4 * g, 1))


def shifts0(ref, x):
    v = ref[x]
    return v, (
        ref[x - 1],
        ref[x + 1],
        pltpu.roll(v, 1, 0),
        pltpu.roll(v, 23, 0),
        pltpu.roll(v, 1, 1),
        pltpu.roll(v, 255, 1),
    )


def coefs_of(k, near):
    faces = [k + n for n in near]
    total = ((faces[0] + faces[1]) + (faces[2] + faces[3])) + (faces[4] + faces[5])
    inv = OMEGA / total
    return [f * inv for f in faces], 0.5 * total


def change(v, near, gs, c):
    t = [g * (n - v) for g, n in zip(gs, near)]
    return c + (((t[0] + t[1]) + (t[2] + t[3])) + (t[4] + t[5]))


def sweep0(cur, out, g, c, low, high):
    def body(x):
        v, near = shifts0(cur, x)
        out[x] = v + change(v, near, [g[i, x] for i in range(6)], c[x])

    layer_loop(low, high, body)


def own_residual0(cur, g, c, t, x):
    v, near = shifts0(cur, x)
    r = change(v, near, [g[i, x] for i in range(6)], c[x]) * t[x]
    return v, r[0:16, 0:128]


def pack1(w, sb, se):
    half, group = lanes_of((8, 128)) < 64, lanes_of((8, 128)) // 8
    for j in range(4):
        sb[j] = jnp.where(half, w[2 * j], w[2 * j + 1])
    for i in range(2):
        z = jnp.zeros((8, 128), F32)
        for x in range(8):
            z = jnp.where(group == x, rot(w[x], 8 * x - 56 * i, 1), z)
        se[i] = jnp.where(half, z, rot(rot(z, 4, 0), 64, 1))[0:4]


def unpack1(w, rb, re, out):
    half, quarter = lanes_of((8, 128)) < 64, lanes_of((8, 128)) < 96

    def block(dx, dy, x):
        if (dx, dy) == (0, 0):
            return w[x]
        tile = rb[PLAN1[(dx, dy, 0)][1] + x // 2 - (1 if dx < 0 else 0)]
        return rot(tile, 64, 1) if x % 2 else tile

    for dx, layers in ((0, range(8)), (1, range(6)), (-1, range(2, 8))):
        for t, dy in enumerate((0, 1, -1)):
            up, lo = re[ENDS1[(dx, dy, 1)][1]], re[ENDS1[(dx, dy, -1)][1]]
            up, lo = (jnp.concatenate([q, rot(q, 64, 1)], axis=0) for q in (up, lo))
            for x in layers:
                ends = jnp.where(quarter, rot(up, 64 - 8 * x, 1), rot(lo, 120 - 8 * x, 1))
                out[6 + x + 8 * dx, 8 * t : 8 * t + 8] = jnp.where(half, block(dx, dy, x), ends)


def shifts1(ref, x):
    v = ref[x]
    return v, (
        ref[x - 1],
        ref[x + 1],
        pltpu.roll(v, 1, 0),
        pltpu.roll(v, 23, 0),
        pltpu.roll(v, 1, 1),
        pltpu.roll(v, 127, 1),
    )


def shifts_round(ref, x, step, lane_step):
    layers, rows = ref.shape[0], ref.shape[1]
    v = ref[x]
    row = rows_of(v.shape)
    below, above = ref[lax.rem(x + layers - step, layers)], ref[lax.rem(x + step, layers)]
    return v, (
        ref[lax.rem(x + layers - 1, layers)],
        ref[lax.rem(x + 1, layers)],
        pltpu.roll(jnp.where(row == rows - 1, below, v), 1, 0),
        pltpu.roll(jnp.where(row == 0, above, v), rows - 1, 0),
        pltpu.roll(v, lane_step, 1),
        pltpu.roll(v, 128 - lane_step, 1),
    )


def pack2(w2, sb):
    group = lanes_of((8, 128)) // 32
    z = w2[0]
    for x in range(1, 4):
        z = jnp.where(group == x, w2[x], z)
    sb[...] = z[0:4]


def unpack2(rb, out):
    group = lanes_of((8, 128)) // 32
    for cx in range(4):
        for t in range(2):
            tiles = {}
            for dz in (-1, 0, 1):
                first = rb[SLOT[(16 * cx + 8 * t + dz) % N]]
                second = rb[SLOT[(16 * cx + 8 * t + 4 + dz) % N]]
                tiles[dz] = jnp.concatenate([first, second], axis=0)
            for x in range(4):
                z = rot(tiles[0], -32 * x, 1)
                z = jnp.where(group == 1, rot(tiles[1], 32 - 32 * x, 1), z)
                z = jnp.where(group == 3, rot(tiles[-1], 96 - 32 * x, 1), z)
                out[4 * cx + x, 8 * t : 8 * t + 8] = z


def pack_parts(main, ends, low, high, sb):
    lane = lanes_of((8, 128))
    inner = main[1]
    outer = jnp.where(lane < 32, main[0], main[5])
    up, lo = low[0], high[0]
    for x in range(1, 4):
        inner = jnp.where(lane // 32 == x, main[x + 1], inner)
    for x in range(1, 6):
        up = jnp.where(lane // 16 == x, low[x], up)
        lo = jnp.where(lane // 16 == x, high[x], lo)
    for x in range(6):
        outer = jnp.where((lane == 97 + 2 * x) | (lane == 112 + 2 * x), ends[x], outer)
        up = jnp.where(lane == 96 + 2 * x, ends[x], up)
        lo = jnp.where(lane == 113 + 2 * x, ends[x], lo)
    for i, tile in enumerate((inner, outer, up, lo)):
        sb[i] = tile


def sum_parts(rb, out):
    lane, row = lanes_of((8, 128)), rows_of((8, 128))
    odd = lane % 2 == 1

    def column(cx, cy):
        first = PART2[(16 * cx + 4 * cy) % N][1]
        inner, outer = rb[first], rb[first + 1]
        up = rb[PART2[(16 * cx + 4 * cy + 1) % N][1]]
        lo = rb[PART2[(16 * cx + 4 * cy - 1) % N][1]]
        above, below = jnp.where(odd, outer, up), jnp.where(odd, lo, outer)
        layers = []
        for x in range(6):
            own = rot(inner, -32 * (x - 1), 1) if 0 < x < 5 else rot(outer, -32 * (x // 5), 1)
            z = jnp.where(lane < 48, rot(up, 32 - 16 * x, 1), rot(lo, 112 - 16 * x, 1))
            z = jnp.where((lane >= 48) & (lane < 112), 0.0, z)
            z = jnp.where(lane < 32, own, z)
            e = jnp.where((lane == 31) | (lane == 32), rot(above, 31 - 96 - 2 * x, 1), 0.0)
            e = jnp.where((lane == 127) | (lane == 0), rot(below, 15 - 2 * x, 1), e)
            layers.append(z + e)
        return layers

    even = {(cx, t): column(cx, 2 * t) for cx in range(4) for t in range(2)}
    turned = {
        (cx, t): [pltpu.roll(q, 4, 0) for q in column(cx, 2 * t + 1)] for cx in range(4) for t in range(2)
    }
    rows = {}
    for cx in range(4):
        for t in range(2):
            after = even[(cx, 1) if t == 0 else ((cx + 1) % 4, 0)]
            before = turned[(cx, 0) if t == 1 else ((cx - 1) % 4, 1)]
            rows[(cx, t)] = [
                jnp.where(row < 5, even[(cx, t)][x], after[x]) + jnp.where(row >= 3, turned[(cx, t)][x], before[x])
                for x in range(6)
            ]
    for cx in range(4):
        for t in range(2):
            for x in range(4):
                z = rows[(cx, t)][x + 1]
                if x == 0:
                    z = z + rows[((cx - 1) % 4, t)][5]
                if x == 3:
                    z = z + rows[((cx + 1) % 4, t)][0]
                out[4 * cx + x, 8 * t : 8 * t + 8] = z


def pair_rows(ref, index, count):
    return ref[index, pl.ds(0, count, stride=2), :] + ref[index, pl.ds(1, count, stride=2), :]


def kernel(
    cls_hbm, val_hbm, cell_hbm, rate_hbm, guess_hbm, p_ref, r_ref,
    cls_ref, val_ref, cell_ref, rate_ref, fr, vb, kf, g0, t0, c0, u0, sb2, rb2, sbv, rbv, se2, re2, sev, rev,
    pair, w1, wk, k1, b1, v1, g1, t1, c1, sbk1, rbk1, sbb1, rbb1, sek1, rek1, seb1, reb1,
    pair1, part, w2, k2, b2, v2, q2, g2, t2, c2, sbk2, rbk2, sbb2, rbb2,
    pair2, k3, v3, q3, g3, t3, c3, exp3, exp2, exp1, send, recv, load,
):
    me = lax.axis_index("space")
    loads = [
        pltpu.make_async_copy(src, dst, load.at[i])
        for i, (src, dst) in enumerate(
            [
                (cls_hbm.at[0], cls_ref),
                (val_hbm, val_ref),
                (guess_hbm.at[0], fr.at[pl.ds(4, 16), pl.ds(0, 16), pl.ds(0, 128)]),
                (cell_hbm, cell_ref),
                (rate_hbm, rate_ref),
            ]
        )
    ]
    for copy in loads:
        copy.start()
    barrier = pltpu.get_barrier_semaphore()
    for o in GATHER:
        pl.semaphore_signal(
            barrier, inc=1, device_id={"space": lax.rem(me + o, N)}, device_id_type=pl.DeviceIdType.MESH
        )

    for copy in loads:
        copy.wait()
    vals = [jnp.broadcast_to(val_ref[0:1, i : i + 1], (16, 128)) for i in range(8)]

    def lookup(x):
        cls = cls_ref[x]
        bits = [(cls & 1) == 0, (cls & 2) == 0, (cls & 4) == 0]
        pairs = [jnp.where(bits[0], vals[2 * i], vals[2 * i + 1]) for i in range(4)]
        quads = [jnp.where(bits[1], pairs[0], pairs[1]), jnp.where(bits[1], pairs[2], pairs[3])]
        kf[x + 4, 0:16, 0:128] = jnp.where(bits[2], quads[0], quads[1])

    layer_loop(0, 16, lookup)
    pack0(lambda a, x: (fr if a == 0 else kf)[x + 4, 0:16, 0:128], 2, sb2, se2)
    pl.semaphore_wait(barrier, len(GATHER))
    send_plan(me, PLAN2, EDGE0, sb2, rb2, se2, re2, send, recv, 0)

    def same(shape, f):
        return f(rows_of(shape), lanes_of(shape)).astype(F32)

    pool0 = same((128, 128), lambda l, c: l // 2 == c % 64)
    pool1 = same((128, 128), lambda l, c: (l // 2 == c % 32) & (l < 64))

    def coarsen0(layer, w1):
        def body(x):
            pair[x] = layer(2 * x) + layer(2 * x + 1)

        layer_loop(0, 8, body)
        sums = jnp.concatenate([pair_rows(pair, x, 8) for x in range(8)], axis=0)
        out = jnp.dot(0.125 * sums, pool0, precision=HI, preferred_element_type=F32)
        for x in range(8):
            w1[x] = out[8 * x : 8 * x + 8]

    def coarsen1(ref, base):
        for x in range(4):
            pair1[x] = ref[base + 2 * x] + ref[base + 2 * x + 1]
        rows = [pair_rows(pair1, x, 4) for x in range(4)]
        sums = jnp.concatenate([q for r in rows for q in (r, r)], axis=0)
        out = jnp.dot(0.125 * sums, pool1, precision=HI, preferred_element_type=F32)
        for x in range(4):
            w2[x] = out[8 * x : 8 * x + 8]

    even = lanes_of((8, 128)) % 2 == 0

    def pool_parts(l, c):
        z = jnp.where(l < 64, l // 2, jnp.where(l < 66, 32, jnp.where(l >= 126, -1, -2)))
        main, ends = z == c % 32, z == jnp.where(c % 2 == 0, -1, 32)
        low, high = z == c % 16, z == 16 + c % 16
        return ((c < 128) & main) | ((c // 128 == 1) & ends) | ((c // 128 == 2) & low) | ((c // 128 == 3) & high)

    def coarsen2(ref, out):
        for x in range(8):
            pair2[x] = ref[2 * x] + ref[2 * x + 1]
        for x in range(8):
            s = 0.125 * pair_rows(pair2, x, 8)
            out[x] = s + jnp.where(even, pltpu.roll(s, 127, 1), pltpu.roll(s, 1, 1))

    coarsen0(lambda x: kf[x + 4, 0:16, 0:128], wk)
    pack1(wk, sbk1, sek1)
    send_plan(me, PLAN1, ENDS1, sbk1, rbk1, sek1, rek1, send, recv, 2)
    coarsen1(wk, 0)
    pack2(w2, sbk2)
    for o in GATHER:
        start_to(me, sbk2, rbk2.at[SLOT[o]], send.at[8], recv.at[8], o)

    cell, rate = cell_ref[...], rate_ref[...]
    ix, iy, iz = cell // (64 * 512), cell // 512 % 64, cell % 512
    theirs = (ix // 16 * 4 + iy // 16) * 4 + iz // 128
    place = lax.rem(theirs - lax.rem(me + ROTATE, N) + 2 * N + 21, N)
    dx, dy, dz = place // 16, place // 4 % 4, place % 4
    fx, fy, fz = ix % 16 + 16 * (dx - 1) + 4, iy % 16 + 16 * (dy - 1), iz % 128 + 128 * (dz - 1)
    held = (dx < 3) & (dy < 3) & (dz < 3) & (fy >= -4) & (fy < 20) & (fz >= -4) & (fz < 132)
    fy, fz = jnp.where(fy < 0, fy + 24, fy), jnp.where(fz < 0, fz + 256, fz)
    rate = jnp.where(held, rate, 0.0)
    in_y = jnp.where(rows_of((24, 16)) == fy, rate, 0.0)
    in_z = jnp.where(rows_of((256, 16)) == fz, 1.0, 0.0)
    left = jnp.concatenate([jnp.where(fx == x, in_y, 0.0) for x in range(24)], axis=0)
    c0[...] = lax.dot_general(
        left, in_z, (((1,), (1,)), ((), ())), precision=HI, preferred_element_type=F32
    ).reshape(24, 24, 256)

    wait_got(rb2, recv.at[0])
    wait_got(re2, recv.at[1])
    unpack0(0, 2, PLAN2, rb2, re2, fr)
    unpack0(1, 2, PLAN2, rb2, re2, kf)

    def coefs0(x):
        k, near = shifts0(kf, x)
        gs, total = coefs_of(k, near)
        for i in range(6):
            g0[i, x] = gs[i]
        t0[x] = (1.0 / OMEGA) * total
        c0[x] = OMEGA * c0[x] / total

    layer_loop(2, 22, coefs0)
    sweep0(fr, vb, g0, c0, 2, 22)
    sweep0(vb, u0, g0, c0, 3, 21)
    coarsen0(lambda x: own_residual0(u0, g0, c0, t0, x + 4)[1], w1)

    pack1(w1, sbb1, seb1)
    send_plan(me, PLAN1, ENDS1, sbb1, rbb1, seb1, reb1, send, recv, 4)

    own1 = lanes_of((8, 128)) < 64

    def part1(x):
        b1[x] = jnp.zeros((24, 128), F32)
        v1[x] = jnp.zeros((24, 128), F32)

    layer_loop(3, 17, part1)
    wait_got(rbk1, recv.at[2])
    wait_got(rek1, recv.at[3])
    unpack1(wk, rbk1, rek1, k1)

    def coefs1(x):
        k, near = shifts1(k1, x)
        gs, total = coefs_of(k, near)
        for i in range(6):
            g1[i, x] = gs[i]
        t1[x] = 0.25 * total

    layer_loop(1, 19, coefs1)
    for x in range(8):
        b1[6 + x, 0:8] = jnp.where(own1, OMEGA * w1[x] / t1[6 + x, 0:8], 0.0)

    def sweep1(cur, out, c, low, high):
        def body(x):
            v, near = shifts1(cur, x)
            out[x] = v + change(v, near, [g1[i, x] for i in range(6)], c[x])

        layer_loop(low, high, body)

    sweep1(b1, v1, b1, 5, 15)
    low4 = rows_of((8, 128)) < 4

    def down1(x):
        v, near = shifts1(v1, x)
        return change(v, near, [g1[i, x] for i in range(6)], b1[x]) * t1[x]

    for i in range(6):
        q = down1(4 + 2 * i) + down1(5 + 2 * i)
        part[i, 0:8] = q[0:8]
        part[i, 8:16] = jnp.where(low4, q[8:16], q[16:24])
    sums = jnp.concatenate([pair_rows(part, x, 8) for x in range(6)], axis=0)
    wide = same((128, 512), pool_parts)
    out = jnp.dot((0.125 / OMEGA) * sums, wide, precision=HI, preferred_element_type=F32)
    pieces = [[out[8 * x : 8 * x + 8, 128 * i : 128 * i + 128] for x in range(6)] for i in range(4)]
    pack_parts(*pieces, sbb2)

    def gather(offsets):
        for o in offsets:
            src, got, count = PART2[o]
            start_to(me, sbb2.at[pl.ds(src, count)], rbb2.at[pl.ds(got, count)], send.at[9], recv.at[9], o)

    gather(GATHER)
    pack0(lambda a, x: u0[x + 4, 0:16, 0:128], 1, sbv, sev)
    send_plan(me, PLANV, EDGE0, sbv, rbv, sev, rev, send, recv, 6)
    for i, buffer in enumerate((rb2, re2, rbk1, rek1)):
        wait_sent(buffer, send.at[i])

    rbk2[SLOT[0]] = sbk2[...]
    wait_got(rbk2.at[pl.ds(0, len(GATHER))], recv.at[8])
    unpack2(rbk2, k2)
    outside = lanes_of((16, 128)) // 32 == 2

    def fill2(x):
        k2[x] = jnp.where(outside, 1.0, k2[x])

    layer_loop(0, 16, fill2)

    def coefs2(x):
        k, near = shifts_round(k2, x, 4, 1)
        gs, total = coefs_of(k, near)
        for i in range(6):
            g2[i, x] = gs[i]
        t2[x] = 0.0625 * total

    layer_loop(0, 16, coefs2)
    coarsen2(k2, k3)

    def coefs3(x):
        k, near = shifts_round(k3, x, 2, 2)
        gs, total = coefs_of(k, near)
        for i in range(6):
            g3[i, x] = gs[i]
        t3[x] = 0.015625 * total

    layer_loop(0, 8, coefs3)

    wait_sent(rbk2.at[pl.ds(0, len(GATHER))], send.at[8])

    wait_got(rbb1, recv.at[4])
    wait_got(reb1, recv.at[5])
    unpack1(w1, rbb1, reb1, b1)

    def first1(x):
        c1[x] = OMEGA * b1[x] / t1[x]

    layer_loop(1, 19, first1)
    sweep1(c1, v1, c1, 2, 18)
    wait_sent(rbb1, send.at[4])
    wait_sent(reb1, send.at[5])

    for i in range(2):
        rbb2[PARTS - 2 + i] = sbb2[i]
    wait_got(rbb2.at[pl.ds(0, PARTS - 2)], recv.at[9])
    sum_parts(rbb2, b2)

    def first2(x):
        c2[x] = OMEGA * jnp.where(outside, 0.0, b2[x]) / t2[x]

    layer_loop(0, 16, first2)

    def sweep2(cur, out):
        def body(x):
            v, near = shifts_round(cur, x, 4, 1)
            out[x] = v + change(v, near, [g2[i, x] for i in range(6)], c2[x])

        layer_loop(0, 16, body)

    sweep2(c2, v2)

    def down2(x):
        v, near = shifts_round(v2, x, 4, 1)
        r = change(v, near, [g2[i, x] for i in range(6)], c2[x]) * t2[x]
        q2[x] = (1.0 / OMEGA) * r

    layer_loop(0, 16, down2)
    coarsen2(q2, c3)

    def first3(x):
        c3[x] = OMEGA * c3[x] / t3[x]

    layer_loop(0, 8, first3)

    def sweep3(cur, out):
        def body(x):
            v, near = shifts_round(cur, x, 2, 2)
            out[x] = v + change(v, near, [g3[i, x] for i in range(6)], c3[x])

        layer_loop(0, 8, body)

    sweep3(c3, v3)
    sweep3(v3, q3)
    sweep3(q3, v3)
    sweep3(v3, q3)
    sweep3(q3, v3)

    def up2(x):
        e = v3[x]
        exp3[x, pl.ds(0, 8, stride=2), :] = e
        exp3[x, pl.ds(1, 8, stride=2), :] = e
        q2[2 * x] = v2[2 * x] + exp3[x]
        q2[2 * x + 1] = v2[2 * x + 1] + exp3[x]

    layer_loop(0, 8, up2)
    sweep2(q2, v2)
    sweep2(v2, q2)

    spread2 = same((128, 128), lambda c, f: c == jnp.where(f < 96, f // 2, 64 + f // 2))
    row = rows_of((8, 128))
    order = [14, 15, 0, 1, 2, 3, 4, 5]
    rows = [jnp.where(row < 6, q2[x, 0:8], q2[(x - 4) % 16, 8:16]) for x in order]
    out = jnp.dot(jnp.concatenate(rows, axis=0), spread2, precision=HI, preferred_element_type=F32)
    for i in range(8):
        e = out[8 * i : 8 * i + 8]
        exp2[i, pl.ds(0, 8, stride=2), :] = e
        exp2[i, pl.ds(1, 8, stride=2), :] = e
    for x in range(2, 18):
        b1[x, 0:16] = v1[x, 0:16] + exp2[(x - 2) // 2]
        b1[x, 16:24] = v1[x, 16:24] + exp2[(x - 2) // 2, 8:16]
    sweep1(b1, v1, c1, 3, 17)
    sweep1(v1, b1, c1, 4, 16)

    wait_got(rbv, recv.at[6])
    wait_got(rev, recv.at[7])
    unpack0(0, 1, PLANV, rbv, rev, u0)
    spread1 = same((128, 256), lambda c, f: c == f // 2)
    rows = [q for x in range(4, 16) for q in (b1[x, 0:8], jnp.where(low4, b1[x, 8:16], b1[x, 16:24]))]
    out = jnp.dot(jnp.concatenate(rows, axis=0), spread1, precision=HI, preferred_element_type=F32)
    for i in range(12):
        for h in range(2):
            e = out[16 * i : 16 * i + 16, 128 * h : 128 * h + 128]
            exp1[i, h, pl.ds(0, 16, stride=2), :] = e
            exp1[i, h, pl.ds(1, 16, stride=2), :] = e
    for i in range(12):
        for h in range(2):
            tail = jnp.where(low4, exp1[i, h, 16:24], exp1[i, h, 24:32])
            for x in (2 * i, 2 * i + 1):
                if 1 <= x < 23:
                    at = pl.ds(128 * h, 128)
                    vb[x, 0:16, at] = u0[x, 0:16, at] + exp1[i, h, 0:16]
                    vb[x, 16:24, at] = u0[x, 16:24, at] + tail
    sweep0(vb, u0, g0, c0, 2, 22)
    sweep0(u0, vb, g0, c0, 3, 21)

    def finish(x):
        v, r = own_residual0(vb, g0, c0, t0, x + 4)
        p_ref[0, x] = v[0:16, 0:128]
        r_ref[0, x] = r

    layer_loop(0, 16, finish)
    wait_sent(rbv, send.at[6])
    wait_sent(rev, send.at[7])
    wait_sent(rbb2.at[pl.ds(0, PARTS - 2)], send.at[9])


def shards(perm_class, class_values, well_cells, well_rates, guess):
    wells = well_cells.shape[0]

    def f(*shape):
        return pltpu.VMEM(shape, F32)

    t = (8, 128)
    l0, l1, l2, l3 = (24, 24, 256), (20, 24, 128), (16, 16, 128), (8, 8, 128)
    vmem = pl.BlockSpec(memory_space=pltpu.VMEM)
    block = jax.ShapeDtypeStruct(guess.shape, F32)
    return pl.pallas_call(
        kernel,
        out_shape=(block, block),
        in_specs=[pl.BlockSpec(memory_space=pltpu.HBM)] * 5,
        out_specs=(vmem, vmem),
        scratch_shapes=[
            pltpu.VMEM(guess.shape[1:], jnp.int32), f(1, 8), pltpu.VMEM((1, wells), jnp.int32), f(1, wells), f(*l0), f(*l0), f(*l0), f(6, *l0), f(*l0), f(*l0), f(*l0),
            f(SEND2, *t), f(GOT2, *t), f(SENDV, *t), f(GOTV, *t), *([f(4, 2, 128), f(len(EDGE0), 2, 128)] * 2),
            f(8, 16, 128), f(8, *t), f(8, *t), f(*l1), f(*l1), f(*l1), f(6, *l1), f(*l1), f(*l1),
            *([f(SEND1, *t), f(GOT1, *t)] * 2), *([f(2, 4, 128), f(len(ENDS1), 4, 128)] * 2),
            f(4, *t), f(6, 16, 128), f(4, *t), f(*l2), f(*l2), f(*l2), f(*l2), f(6, *l2), f(*l2), f(*l2),
            f(4, 128), f(len(GATHER) + 1, 4, 128), f(4, *t), f(PARTS, *t),
            f(8, 16, 128), f(*l3), f(*l3), f(*l3), f(6, *l3), f(*l3), f(*l3),
            f(8, 16, 128), f(8, 16, 128), f(12, 2, 32, 128),
            pltpu.SemaphoreType.DMA((10,)), pltpu.SemaphoreType.DMA((10,)), pltpu.SemaphoreType.DMA((5,)),
        ],
        compiler_params=pltpu.CompilerParams(
            collective_id=0, has_side_effects=True, vmem_limit_bytes=40 * 1024 * 1024
        ),
    )(*[pltpu.with_memory_space_constraint(q, pltpu.HBM) for q in (perm_class, class_values.reshape(1, 8), well_cells.reshape(1, wells), well_rates.reshape(1, wells), guess)])


def solution(mesh):
    whole = P(("real", "space"), None, None, None)
    return jax.shard_map(
        shards,
        mesh=mesh,
        in_specs=(P("space", None, None, None), P(), P("real"), P("real"), whole),
        out_specs=(whole, whole),
        check_vma=False,
    )
```

```python
import functools

import jax
import jax.numpy as jnp
from jax import lax
from jax.experimental import pallas as pl
from jax.experimental.pallas import tpu as pltpu
from jax.sharding import PartitionSpec as P

N = 64
ROTATE = 21
OMEGA = 0.8
F32 = jnp.float32
HI = lax.Precision.HIGHEST
DIRS = [(a, b, c) for a in (-1, 0, 1) for b in (-1, 0, 1) for c in (-1, 0, 1) if (a, b, c) != (0, 0, 0)]


def offset(d):
    return (16 * d[0] + 4 * d[1] + d[2]) % N


def hops(off):
    total = 0
    for row in range(N):
        to = (row + off) % N
        y, z = abs(row // 16 - to // 16), abs(row // 2 % 8 - to // 2 % 8)
        total += min(y, 4 - y) + min(z, 8 - z) + 2 * abs(row % 2 - to % 2)
    return total


def sent0(narr):
    x_at = {1: 0, -1: 6 * narr}
    y_at = {1: 12 * narr, -1: 20 * narr}
    e_at = {d: 28 * narr + i for i, d in enumerate([(1, 1), (1, -1), (-1, 1), (-1, -1)])}
    z_at = {1: 28 * narr + 4, -1: 29 * narr + 4}
    return x_at, y_at, e_at, z_at, 30 * narr + 4


def plan0(narr):
    x_at, y_at, e_at, z_at, length = sent0(narr)
    plan, got = {}, 0
    for d in DIRS:
        dx, dy, dz = d
        if dy and dz:
            continue
        if dz:
            src, count = z_at[dz], narr
        elif dx and dy:
            src, count = e_at[(dx, dy)], 1
        elif dy:
            src, count = y_at[dy], 8 * narr
        else:
            src, count = x_at[dx], 6 * narr
        plan[d] = (src, got, count)
        got += count
    return plan, length, got


def plan1():
    plan, got = {}, 0
    for d in DIRS:
        dx, dy, dz = d
        if dz:
            continue
        src, count = (1 if dx < 0 else 0, 3) if dx else (0, 4)
        plan[d] = (src, got, count)
        got += count
    return plan, 4, got


PLAN2, SEND2, GOT2 = plan0(2)
PLANV, SENDV, GOTV = plan0(1)
PLAN1, SEND1, GOT1 = plan1()
SIDE2 = {(dz, dy): i for i, (dz, dy) in enumerate([(1, 1), (1, -1), (-1, 1), (-1, -1)])}
EDGE0 = {d: (SIDE2[(d[2], d[1])], i, 1) for i, d in enumerate(d for d in DIRS if d[1] and d[2])}
ENDS1 = {d: ((1 - d[2]) // 2, i, 1) for i, d in enumerate(d for d in DIRS if d[2])}
NEAR = sorted((offset(d) for d in DIRS), key=lambda o: (-hops(o), o))
GATHER = sorted((o for o in range(1, N) if o % 4 != 2), key=lambda o: (o % 4 == 0, -hops(o), o))
SLOT = {o: i for i, o in enumerate(GATHER)}
SLOT[0] = len(GATHER)


def plan2():
    places, got = {}, 0
    for o in GATHER + [0]:
        side = {0: 0, 1: 1, 3: -1}[o % 4]
        places[o] = (0, got, 2) if side == 0 else (2 if side > 0 else 3, got, 1)
        got += places[o][2]
    return places, got


PART2, PARTS = plan2()


def rows_of(shape):
    return lax.broadcasted_iota(jnp.int32, shape, len(shape) - 2)


def lanes_of(shape):
    return lax.broadcasted_iota(jnp.int32, shape, len(shape) - 1)


def rot(v, by, axis):
    by %= v.shape[axis]
    return pltpu.roll(v, by, axis) if by else v


def layer_loop(low, high, body, unroll=None):
    def step(x, carry):
        body(x)
        return carry

    lax.fori_loop(low, high, step, 0, unroll=unroll or high - low)


def start_to(me, src, dst, send, recv, off):
    pltpu.make_async_remote_copy(
        src_ref=src,
        dst_ref=dst,
        send_sem=send,
        recv_sem=recv,
        device_id={"space": lax.rem(me + (N - off) % N, N)},
        device_id_type=pl.DeviceIdType.MESH,
    ).start()


def send_plan(me, plan, small, sb, rb, se, re, send, recv, i):
    for d in sorted(DIRS, key=lambda d: -hops(offset(d))):
        for messages, src, dst, sem in ((plan, sb, rb, i), (small, se, re, i + 1)):
            if d in messages:
                first, got, count = messages[d]
                start_to(
                    me, src.at[pl.ds(first, count)], dst.at[pl.ds(got, count)], send.at[sem], recv.at[sem], offset(d)
                )


def wait_got(rb, recv):
    pltpu.make_async_copy(rb, rb, recv).wait()


def wait_sent(rb, send):
    pltpu.make_async_copy(rb, rb, send).wait()


def pack0(own, narr, sb, se):
    x_at, y_at, e_at, z_at, _ = sent0(narr)
    low4 = rows_of((8, 128)) < 4
    two = rows_of((8, 128)) // 2
    group = lanes_of((16, 128)) // 4
    zlo = zhi = jnp.zeros((16, 128), F32)
    for a in range(narr):
        for i in range(3):
            for side, x in ((1, i), (-1, 13 + i)):
                v = own(a, x)
                sb[x_at[side] + a * 6 + 2 * i] = v[0:8]
                sb[x_at[side] + a * 6 + 2 * i + 1] = v[8:16]
        for i in range(8):
            v, w = own(a, i), own(a, i + 8)
            sb[y_at[1] + i * narr + a] = jnp.where(low4, v[0:8], rot(w[0:8], 4, 0))
            sb[y_at[-1] + i * narr + a] = jnp.where(low4, rot(w[8:16], 4, 0), v[8:16])
    for (dx, dy), at in e_at.items():
        z = jnp.zeros((8, 128), F32)
        for a in range(narr):
            for i in range(2):
                v = own(a, i if dx > 0 else 14 + i)
                v = v[0:8] if dy > 0 else v[8:16]
                z = jnp.where(two == 2 * a + i, rot(v, 4 * a + 2 * i - (0 if dy > 0 else 6), 0), z)
        sb[at] = z
    for a in range(narr):
        for x in range(16):
            v, g = own(a, x), 16 * a + x
            zlo = jnp.where(group == g, rot(v, 4 * g, 1), zlo)
            zhi = jnp.where(group == g, rot(v, 4 * g + 4, 1), zhi)
    for side, z in ((1, zlo), (-1, zhi)):
        if narr == 2:
            sb[z_at[side]] = z[0:8]
            sb[z_at[side] + 1] = z[8:16]
        else:
            sb[z_at[side]] = jnp.where(lanes_of((8, 128)) < 64, z[0:8], rot(z[8:16], 64, 1))
        se[SIDE2[(side, 1)]] = z[0:2]
        se[SIDE2[(side, -1)]] = z[14:16]


def unpack0(a, narr, plan, rb, re, out):
    low4 = rows_of((8, 128)) < 4

    def at(d):
        return plan[d][1]

    for i in range(3):
        for dx, base in ((1, 20), (-1, 1)):
            first = at((dx, 0, 0)) + a * 6 + 2 * i
            out[base + i, 0:8, 0:128] = rb[first]
            out[base + i, 8:16, 0:128] = rb[first + 1]
    for i in range(8):
        up, lo = rb[at((0, 1, 0)) + i * narr + a], rb[at((0, -1, 0)) + i * narr + a]
        out[4 + i, 16:24, 0:128] = jnp.where(low4, up, lo)
        out[12 + i, 16:24, 0:128] = rot(jnp.where(low4, lo, up), 4, 0)
    for dx, base in ((1, 20), (-1, 2)):
        for i in range(2):
            up = rot(rb[at((dx, 1, 0))], -(4 * a + 2 * i), 0)
            lo = rot(rb[at((dx, -1, 0))], 6 - (4 * a + 2 * i), 0)
            out[base + i, 16:24, 0:128] = jnp.where(low4, up, lo)
    half = lanes_of((24, 128)) < 64
    for dx, layers in ((0, range(4, 20)), (1, range(20, 23)), (-1, range(1, 4))):
        parts = {}
        for dz in (1, -1):
            mid = at((dx, 0, dz))
            up, lo = re[EDGE0[(dx, 1, dz)][1]], re[EDGE0[(dx, -1, dz)][1]]
            last = rb[mid + 1] if narr == 2 else rot(rb[mid], 64, 1)
            parts[dz] = jnp.concatenate([rb[mid], last, up, up, lo, lo], axis=0)
        for x in layers:
            g = 16 * a + (x - 4) % 16
            out[x, :, 128:256] = jnp.where(half, rot(parts[1], -4 * g, 1), rot(parts[-1], 124 - 4 * g, 1))


def shifts0(ref, x):
    v = ref[x]
    return v, (
        ref[x - 1],
        ref[x + 1],
        pltpu.roll(v, 1, 0),
        pltpu.roll(v, 23, 0),
        pltpu.roll(v, 1, 1),
        pltpu.roll(v, 255, 1),
    )


def coefs_of(k, near):
    faces = [k + n for n in near]
    total = ((faces[0] + faces[1]) + (faces[2] + faces[3])) + (faces[4] + faces[5])
    inv = OMEGA / total
    return [f * inv for f in faces], 0.5 * total


def change(v, near, gs, c):
    t = [g * (n - v) for g, n in zip(gs, near)]
    return c + (((t[0] + t[1]) + (t[2] + t[3])) + (t[4] + t[5]))


def sweep0(cur, out, g, c, low, high):
    def body(x):
        v, near = shifts0(cur, x)
        out[x] = v + change(v, near, [g[i, x] for i in range(6)], c[x])

    layer_loop(low, high, body)


def own_residual0(cur, g, c, t, x):
    v, near = shifts0(cur, x)
    r = change(v, near, [g[i, x] for i in range(6)], c[x]) * t[x]
    return v, r[0:16, 0:128]


def pack1(w, sb, se):
    half, group = lanes_of((8, 128)) < 64, lanes_of((8, 128)) // 8
    for j in range(4):
        sb[j] = jnp.where(half, w[2 * j], w[2 * j + 1])
    for i in range(2):
        z = jnp.zeros((8, 128), F32)
        for x in range(8):
            z = jnp.where(group == x, rot(w[x], 8 * x - 56 * i, 1), z)
        se[i] = jnp.where(half, z, rot(rot(z, 4, 0), 64, 1))[0:4]


def unpack1(w, rb, re, out):
    half, quarter = lanes_of((8, 128)) < 64, lanes_of((8, 128)) < 96

    def block(dx, dy, x):
        if (dx, dy) == (0, 0):
            return w[x]
        tile = rb[PLAN1[(dx, dy, 0)][1] + x // 2 - (1 if dx < 0 else 0)]
        return rot(tile, 64, 1) if x % 2 else tile

    for dx, layers in ((0, range(8)), (1, range(6)), (-1, range(2, 8))):
        for t, dy in enumerate((0, 1, -1)):
            up, lo = re[ENDS1[(dx, dy, 1)][1]], re[ENDS1[(dx, dy, -1)][1]]
            up, lo = (jnp.concatenate([q, rot(q, 64, 1)], axis=0) for q in (up, lo))
            for x in layers:
                ends = jnp.where(quarter, rot(up, 64 - 8 * x, 1), rot(lo, 120 - 8 * x, 1))
                out[6 + x + 8 * dx, 8 * t : 8 * t + 8] = jnp.where(half, block(dx, dy, x), ends)


def shifts1(ref, x):
    v = ref[x]
    return v, (
        ref[x - 1],
        ref[x + 1],
        pltpu.roll(v, 1, 0),
        pltpu.roll(v, 23, 0),
        pltpu.roll(v, 1, 1),
        pltpu.roll(v, 127, 1),
    )


def shifts_round(ref, x, step, lane_step):
    layers, rows = ref.shape[0], ref.shape[1]
    v = ref[x]
    row = rows_of(v.shape)
    below, above = ref[lax.rem(x + layers - step, layers)], ref[lax.rem(x + step, layers)]
    return v, (
        ref[lax.rem(x + layers - 1, layers)],
        ref[lax.rem(x + 1, layers)],
        pltpu.roll(jnp.where(row == rows - 1, below, v), 1, 0),
        pltpu.roll(jnp.where(row == 0, above, v), rows - 1, 0),
        pltpu.roll(v, lane_step, 1),
        pltpu.roll(v, 128 - lane_step, 1),
    )


def pack2(w2, sb):
    group = lanes_of((8, 128)) // 32
    z = w2[0]
    for x in range(1, 4):
        z = jnp.where(group == x, w2[x], z)
    sb[...] = z[0:4]


def unpack2(rb, out):
    group = lanes_of((8, 128)) // 32
    for cx in range(4):
        for t in range(2):
            tiles = {}
            for dz in (-1, 0, 1):
                first = rb[SLOT[(16 * cx + 8 * t + dz) % N]]
                second = rb[SLOT[(16 * cx + 8 * t + 4 + dz) % N]]
                tiles[dz] = jnp.concatenate([first, second], axis=0)
            for x in range(4):
                z = rot(tiles[0], -32 * x, 1)
                z = jnp.where(group == 1, rot(tiles[1], 32 - 32 * x, 1), z)
                z = jnp.where(group == 3, rot(tiles[-1], 96 - 32 * x, 1), z)
                out[4 * cx + x, 8 * t : 8 * t + 8] = z


def pack_parts(main, ends, low, high, sb):
    lane = lanes_of((8, 128))
    inner = main[1]
    outer = jnp.where(lane < 32, main[0], main[5])
    up, lo = low[0], high[0]
    for x in range(1, 4):
        inner = jnp.where(lane // 32 == x, main[x + 1], inner)
    for x in range(1, 6):
        up = jnp.where(lane // 16 == x, low[x], up)
        lo = jnp.where(lane // 16 == x, high[x], lo)
    for x in range(6):
        outer = jnp.where((lane == 97 + 2 * x) | (lane == 112 + 2 * x), ends[x], outer)
        up = jnp.where(lane == 96 + 2 * x, ends[x], up)
        lo = jnp.where(lane == 113 + 2 * x, ends[x], lo)
    for i, tile in enumerate((inner, outer, up, lo)):
        sb[i] = tile


def sum_parts(rb, out):
    lane, row = lanes_of((8, 128)), rows_of((8, 128))
    odd = lane % 2 == 1

    def column(cx, cy):
        first = PART2[(16 * cx + 4 * cy) % N][1]
        inner, outer = rb[first], rb[first + 1]
        up = rb[PART2[(16 * cx + 4 * cy + 1) % N][1]]
        lo = rb[PART2[(16 * cx + 4 * cy - 1) % N][1]]
        above, below = jnp.where(odd, outer, up), jnp.where(odd, lo, outer)
        layers = []
        for x in range(6):
            own = rot(inner, -32 * (x - 1), 1) if 0 < x < 5 else rot(outer, -32 * (x // 5), 1)
            z = jnp.where(lane < 48, rot(up, 32 - 16 * x, 1), rot(lo, 112 - 16 * x, 1))
            z = jnp.where((lane >= 48) & (lane < 112), 0.0, z)
            z = jnp.where(lane < 32, own, z)
            e = jnp.where((lane == 31) | (lane == 32), rot(above, 31 - 96 - 2 * x, 1), 0.0)
            e = jnp.where((lane == 127) | (lane == 0), rot(below, 15 - 2 * x, 1), e)
            layers.append(z + e)
        return layers

    even = {(cx, t): column(cx, 2 * t) for cx in range(4) for t in range(2)}
    turned = {
        (cx, t): [pltpu.roll(q, 4, 0) for q in column(cx, 2 * t + 1)] for cx in range(4) for t in range(2)
    }
    rows = {}
    for cx in range(4):
        for t in range(2):
            after = even[(cx, 1) if t == 0 else ((cx + 1) % 4, 0)]
            before = turned[(cx, 0) if t == 1 else ((cx - 1) % 4, 1)]
            rows[(cx, t)] = [
                jnp.where(row < 5, even[(cx, t)][x], after[x]) + jnp.where(row >= 3, turned[(cx, t)][x], before[x])
                for x in range(6)
            ]
    for cx in range(4):
        for t in range(2):
            for x in range(4):
                z = rows[(cx, t)][x + 1]
                if x == 0:
                    z = z + rows[((cx - 1) % 4, t)][5]
                if x == 3:
                    z = z + rows[((cx + 1) % 4, t)][0]
                out[4 * cx + x, 8 * t : 8 * t + 8] = z


def pair_rows(ref, index, count):
    return ref[index, pl.ds(0, count, stride=2), :] + ref[index, pl.ds(1, count, stride=2), :]


def kernel(
    cls_hbm, val_hbm, cell_hbm, rate_hbm, guess_hbm, p_ref, r_ref,
    cls_ref, val_ref, cell_ref, rate_ref, fr, vb, kf, g0, t0, c0, u0, sb2, rb2, sbv, rbv, se2, re2, sev, rev,
    pair, w1, wk, k1, b1, v1, g1, t1, c1, sbk1, rbk1, sbb1, rbb1, sek1, rek1, seb1, reb1,
    pair1, part, w2, k2, b2, v2, q2, g2, t2, c2, sbk2, rbk2, sbb2, rbb2,
    pair2, k3, v3, q3, g3, t3, c3, exp3, exp2, exp1, send, recv, load,
):
    me = lax.axis_index("space")
    loads = [
        pltpu.make_async_copy(src, dst, load.at[i])
        for i, (src, dst) in enumerate(
            [
                (cls_hbm.at[0], cls_ref),
                (val_hbm, val_ref),
                (guess_hbm.at[0], fr.at[pl.ds(4, 16), pl.ds(0, 16), pl.ds(0, 128)]),
                (cell_hbm, cell_ref),
                (rate_hbm, rate_ref),
            ]
        )
    ]
    for copy in loads:
        copy.start()
    barrier = pltpu.get_barrier_semaphore()
    for o in GATHER:
        pl.semaphore_signal(
            barrier, inc=1, device_id={"space": lax.rem(me + o, N)}, device_id_type=pl.DeviceIdType.MESH
        )

    for copy in loads:
        copy.wait()
    vals = [jnp.broadcast_to(val_ref[0:1, i : i + 1], (16, 128)) for i in range(8)]

    def lookup(x):
        cls = cls_ref[x]
        bits = [(cls & 1) == 0, (cls & 2) == 0, (cls & 4) == 0]
        pairs = [jnp.where(bits[0], vals[2 * i], vals[2 * i + 1]) for i in range(4)]
        quads = [jnp.where(bits[1], pairs[0], pairs[1]), jnp.where(bits[1], pairs[2], pairs[3])]
        kf[x + 4, 0:16, 0:128] = jnp.where(bits[2], quads[0], quads[1])

    layer_loop(0, 16, lookup)
    pack0(lambda a, x: (fr if a == 0 else kf)[x + 4, 0:16, 0:128], 2, sb2, se2)
    pl.semaphore_wait(barrier, len(GATHER))
    send_plan(me, PLAN2, EDGE0, sb2, rb2, se2, re2, send, recv, 0)

    def same(shape, f):
        return f(rows_of(shape), lanes_of(shape)).astype(F32)

    pool0 = same((128, 128), lambda l, c: l // 2 == c % 64)
    pool1 = same((128, 128), lambda l, c: (l // 2 == c % 32) & (l < 64))

    def coarsen0(layer, w1):
        def body(x):
            pair[x] = layer(2 * x) + layer(2 * x + 1)

        layer_loop(0, 8, body)
        sums = jnp.concatenate([pair_rows(pair, x, 8) for x in range(8)], axis=0)
        out = jnp.dot(0.125 * sums, pool0, precision=HI, preferred_element_type=F32)
        for x in range(8):
            w1[x] = out[8 * x : 8 * x + 8]

    def coarsen1(ref, base):
        for x in range(4):
            pair1[x] = ref[base + 2 * x] + ref[base + 2 * x + 1]
        rows = [pair_rows(pair1, x, 4) for x in range(4)]
        sums = jnp.concatenate([q for r in rows for q in (r, r)], axis=0)
        out = jnp.dot(0.125 * sums, pool1, precision=HI, preferred_element_type=F32)
        for x in range(4):
            w2[x] = out[8 * x : 8 * x + 8]

    even = lanes_of((8, 128)) % 2 == 0

    def pool_parts(l, c):
        z = jnp.where(l < 64, l // 2, jnp.where(l < 66, 32, jnp.where(l >= 126, -1, -2)))
        main, ends = z == c % 32, z == jnp.where(c % 2 == 0, -1, 32)
        low, high = z == c % 16, z == 16 + c % 16
        return ((c < 128) & main) | ((c // 128 == 1) & ends) | ((c // 128 == 2) & low) | ((c // 128 == 3) & high)

    def coarsen2(ref, out):
        for x in range(8):
            pair2[x] = ref[2 * x] + ref[2 * x + 1]
        for x in range(8):
            s = 0.125 * pair_rows(pair2, x, 8)
            out[x] = s + jnp.where(even, pltpu.roll(s, 127, 1), pltpu.roll(s, 1, 1))

    coarsen0(lambda x: kf[x + 4, 0:16, 0:128], wk)
    pack1(wk, sbk1, sek1)
    send_plan(me, PLAN1, ENDS1, sbk1, rbk1, sek1, rek1, send, recv, 2)
    coarsen1(wk, 0)
    pack2(w2, sbk2)
    for o in GATHER:
        start_to(me, sbk2, rbk2.at[SLOT[o]], send.at[8], recv.at[8], o)

    cell, rate = cell_ref[...], rate_ref[...]
    ix, iy, iz = cell // (64 * 512), cell // 512 % 64, cell % 512
    theirs = (ix // 16 * 4 + iy // 16) * 4 + iz // 128
    place = lax.rem(theirs - lax.rem(me + ROTATE, N) + 2 * N + 21, N)
    dx, dy, dz = place // 16, place // 4 % 4, place % 4
    fx, fy, fz = ix % 16 + 16 * (dx - 1) + 4, iy % 16 + 16 * (dy - 1), iz % 128 + 128 * (dz - 1)
    held = (dx < 3) & (dy < 3) & (dz < 3) & (fy >= -4) & (fy < 20) & (fz >= -4) & (fz < 132)
    fy, fz = jnp.where(fy < 0, fy + 24, fy), jnp.where(fz < 0, fz + 256, fz)
    rate = jnp.where(held, rate, 0.0)
    in_y = jnp.where(rows_of((24, 16)) == fy, rate, 0.0)
    in_z = jnp.where(rows_of((256, 16)) == fz, 1.0, 0.0)
    left = jnp.concatenate([jnp.where(fx == x, in_y, 0.0) for x in range(24)], axis=0)
    c0[...] = lax.dot_general(
        left, in_z, (((1,), (1,)), ((), ())), precision=HI, preferred_element_type=F32
    ).reshape(24, 24, 256)

    wait_got(rb2, recv.at[0])
    wait_got(re2, recv.at[1])
    unpack0(0, 2, PLAN2, rb2, re2, fr)
    unpack0(1, 2, PLAN2, rb2, re2, kf)

    def coefs0(x):
        k, near = shifts0(kf, x)
        gs, total = coefs_of(k, near)
        for i in range(6):
            g0[i, x] = gs[i]
        t0[x] = (1.0 / OMEGA) * total
        c0[x] = OMEGA * c0[x] / total

    layer_loop(2, 22, coefs0)
    sweep0(fr, vb, g0, c0, 2, 22)
    sweep0(vb, u0, g0, c0, 3, 21)
    coarsen0(lambda x: own_residual0(u0, g0, c0, t0, x + 4)[1], w1)

    pack1(w1, sbb1, seb1)
    send_plan(me, PLAN1, ENDS1, sbb1, rbb1, seb1, reb1, send, recv, 4)

    own1 = lanes_of((8, 128)) < 64

    def part1(x):
        b1[x] = jnp.zeros((24, 128), F32)
        v1[x] = jnp.zeros((24, 128), F32)

    layer_loop(3, 17, part1)
    wait_got(rbk1, recv.at[2])
    wait_got(rek1, recv.at[3])
    unpack1(wk, rbk1, rek1, k1)

    def coefs1(x):
        k, near = shifts1(k1, x)
        gs, total = coefs_of(k, near)
        for i in range(6):
            g1[i, x] = gs[i]
        t1[x] = 0.25 * total

    layer_loop(1, 19, coefs1)
    for x in range(8):
        b1[6 + x, 0:8] = jnp.where(own1, OMEGA * w1[x] / t1[6 + x, 0:8], 0.0)

    def sweep1(cur, out, c, low, high):
        def body(x):
            v, near = shifts1(cur, x)
            out[x] = v + change(v, near, [g1[i, x] for i in range(6)], c[x])

        layer_loop(low, high, body)

    sweep1(b1, v1, b1, 5, 15)
    low4 = rows_of((8, 128)) < 4

    def down1(x):
        v, near = shifts1(v1, x)
        return change(v, near, [g1[i, x] for i in range(6)], b1[x]) * t1[x]

    for i in range(6):
        q = down1(4 + 2 * i) + down1(5 + 2 * i)
        part[i, 0:8] = q[0:8]
        part[i, 8:16] = jnp.where(low4, q[8:16], q[16:24])
    sums = jnp.concatenate([pair_rows(part, x, 8) for x in range(6)], axis=0)
    wide = same((128, 512), pool_parts)
    out = jnp.dot((0.125 / OMEGA) * sums, wide, precision=HI, preferred_element_type=F32)
    pieces = [[out[8 * x : 8 * x + 8, 128 * i : 128 * i + 128] for x in range(6)] for i in range(4)]
    pack_parts(*pieces, sbb2)

    def gather(offsets):
        for o in offsets:
            src, got, count = PART2[o]
            start_to(me, sbb2.at[pl.ds(src, count)], rbb2.at[pl.ds(got, count)], send.at[9], recv.at[9], o)

    gather(GATHER)
    pack0(lambda a, x: u0[x + 4, 0:16, 0:128], 1, sbv, sev)
    send_plan(me, PLANV, EDGE0, sbv, rbv, sev, rev, send, recv, 6)
    for i, buffer in enumerate((rb2, re2, rbk1, rek1)):
        wait_sent(buffer, send.at[i])

    rbk2[SLOT[0]] = sbk2[...]
    wait_got(rbk2.at[pl.ds(0, len(GATHER))], recv.at[8])
    unpack2(rbk2, k2)
    outside = lanes_of((16, 128)) // 32 == 2

    def fill2(x):
        k2[x] = jnp.where(outside, 1.0, k2[x])

    layer_loop(0, 16, fill2)

    def coefs2(x):
        k, near = shifts_round(k2, x, 4, 1)
        gs, total = coefs_of(k, near)
        for i in range(6):
            g2[i, x] = gs[i]
        t2[x] = 0.0625 * total

    layer_loop(0, 16, coefs2)
    coarsen2(k2, k3)

    def coefs3(x):
        k, near = shifts_round(k3, x, 2, 2)
        gs, total = coefs_of(k, near)
        for i in range(6):
            g3[i, x] = gs[i]
        t3[x] = 0.015625 * total

    layer_loop(0, 8, coefs3)

    wait_sent(rbk2.at[pl.ds(0, len(GATHER))], send.at[8])

    wait_got(rbb1, recv.at[4])
    wait_got(reb1, recv.at[5])
    unpack1(w1, rbb1, reb1, b1)

    def first1(x):
        c1[x] = OMEGA * b1[x] / t1[x]

    layer_loop(1, 19, first1)
    sweep1(c1, v1, c1, 2, 18)
    wait_sent(rbb1, send.at[4])
    wait_sent(reb1, send.at[5])

    for i in range(2):
        rbb2[PARTS - 2 + i] = sbb2[i]
    wait_got(rbb2.at[pl.ds(0, PARTS - 2)], recv.at[9])
    sum_parts(rbb2, b2)

    def first2(x):
        c2[x] = OMEGA * jnp.where(outside, 0.0, b2[x]) / t2[x]

    layer_loop(0, 16, first2)

    def sweep2(cur, out):
        def body(x):
            v, near = shifts_round(cur, x, 4, 1)
            out[x] = v + change(v, near, [g2[i, x] for i in range(6)], c2[x])

        layer_loop(0, 16, body)

    sweep2(c2, v2)

    def down2(x):
        v, near = shifts_round(v2, x, 4, 1)
        r = change(v, near, [g2[i, x] for i in range(6)], c2[x]) * t2[x]
        q2[x] = (1.0 / OMEGA) * r

    layer_loop(0, 16, down2)
    coarsen2(q2, c3)

    def first3(x):
        c3[x] = OMEGA * c3[x] / t3[x]

    layer_loop(0, 8, first3)

    def sweep3(cur, out):
        def body(x):
            v, near = shifts_round(cur, x, 2, 2)
            out[x] = v + change(v, near, [g3[i, x] for i in range(6)], c3[x])

        layer_loop(0, 8, body)

    sweep3(c3, v3)
    sweep3(v3, q3)
    sweep3(q3, v3)
    sweep3(v3, q3)
    sweep3(q3, v3)

    def up2(x):
        e = v3[x]
        exp3[x, pl.ds(0, 8, stride=2), :] = e
        exp3[x, pl.ds(1, 8, stride=2), :] = e
        q2[2 * x] = v2[2 * x] + exp3[x]
        q2[2 * x + 1] = v2[2 * x + 1] + exp3[x]

    layer_loop(0, 8, up2)
    sweep2(q2, v2)
    sweep2(v2, q2)

    spread2 = same((128, 128), lambda c, f: c == jnp.where(f < 96, f // 2, 64 + f // 2))
    row = rows_of((8, 128))
    order = [14, 15, 0, 1, 2, 3, 4, 5]
    rows = [jnp.where(row < 6, q2[x, 0:8], q2[(x - 4) % 16, 8:16]) for x in order]
    out = jnp.dot(jnp.concatenate(rows, axis=0), spread2, precision=HI, preferred_element_type=F32)
    for i in range(8):
        e = out[8 * i : 8 * i + 8]
        exp2[i, pl.ds(0, 8, stride=2), :] = e
        exp2[i, pl.ds(1, 8, stride=2), :] = e
    for x in range(2, 18):
        b1[x, 0:16] = v1[x, 0:16] + exp2[(x - 2) // 2]
        b1[x, 16:24] = v1[x, 16:24] + exp2[(x - 2) // 2, 8:16]
    sweep1(b1, v1, c1, 3, 17)
    sweep1(v1, b1, c1, 4, 16)

    wait_got(rbv, recv.at[6])
    wait_got(rev, recv.at[7])
    unpack0(0, 1, PLANV, rbv, rev, u0)
    spread1 = same((128, 256), lambda c, f: c == f // 2)
    rows = [q for x in range(4, 16) for q in (b1[x, 0:8], jnp.where(low4, b1[x, 8:16], b1[x, 16:24]))]
    out = jnp.dot(jnp.concatenate(rows, axis=0), spread1, precision=HI, preferred_element_type=F32)
    for i in range(12):
        for h in range(2):
            e = out[16 * i : 16 * i + 16, 128 * h : 128 * h + 128]
            exp1[i, h, pl.ds(0, 16, stride=2), :] = e
            exp1[i, h, pl.ds(1, 16, stride=2), :] = e
    for i in range(12):
        for h in range(2):
            tail = jnp.where(low4, exp1[i, h, 16:24], exp1[i, h, 24:32])
            for x in (2 * i, 2 * i + 1):
                if 1 <= x < 23:
                    at = pl.ds(128 * h, 128)
                    vb[x, 0:16, at] = u0[x, 0:16, at] + exp1[i, h, 0:16]
                    vb[x, 16:24, at] = u0[x, 16:24, at] + tail
    sweep0(vb, u0, g0, c0, 2, 22)
    sweep0(u0, vb, g0, c0, 3, 21)

    def finish(x):
        v, r = own_residual0(vb, g0, c0, t0, x + 4)
        p_ref[0, x] = v[0:16, 0:128]
        r_ref[0, x] = r

    layer_loop(0, 16, finish)
    wait_sent(rbv, send.at[6])
    wait_sent(rev, send.at[7])
    wait_sent(rbb2.at[pl.ds(0, PARTS - 2)], send.at[9])


def shards(perm_class, class_values, well_cells, well_rates, guess):
    wells = well_cells.shape[0]

    def f(*shape):
        return pltpu.VMEM(shape, F32)

    t = (8, 128)
    l0, l1, l2, l3 = (24, 24, 256), (20, 24, 128), (16, 16, 128), (8, 8, 128)
    vmem = pl.BlockSpec(memory_space=pltpu.VMEM)
    block = jax.ShapeDtypeStruct(guess.shape, F32)
    return pl.pallas_call(
        kernel,
        out_shape=(block, block),
        in_specs=[pl.BlockSpec(memory_space=pltpu.HBM)] * 5,
        out_specs=(vmem, vmem),
        scratch_shapes=[
            pltpu.VMEM(guess.shape[1:], jnp.int32), f(1, 8), pltpu.VMEM((1, wells), jnp.int32), f(1, wells), f(*l0), f(*l0), f(*l0), f(6, *l0), f(*l0), f(*l0), f(*l0),
            f(SEND2, *t), f(GOT2, *t), f(SENDV, *t), f(GOTV, *t), *([f(4, 2, 128), f(len(EDGE0), 2, 128)] * 2),
            f(8, 16, 128), f(8, *t), f(8, *t), f(*l1), f(*l1), f(*l1), f(6, *l1), f(*l1), f(*l1),
            *([f(SEND1, *t), f(GOT1, *t)] * 2), *([f(2, 4, 128), f(len(ENDS1), 4, 128)] * 2),
            f(4, *t), f(6, 16, 128), f(4, *t), f(*l2), f(*l2), f(*l2), f(*l2), f(6, *l2), f(*l2), f(*l2),
            f(4, 128), f(len(GATHER) + 1, 4, 128), f(4, *t), f(PARTS, *t),
            f(8, 16, 128), f(*l3), f(*l3), f(*l3), f(6, *l3), f(*l3), f(*l3),
            f(8, 16, 128), f(8, 16, 128), f(12, 2, 32, 128),
            pltpu.SemaphoreType.DMA((10,)), pltpu.SemaphoreType.DMA((10,)), pltpu.SemaphoreType.DMA((5,)),
        ],
        compiler_params=pltpu.CompilerParams(
            collective_id=0, has_side_effects=True, vmem_limit_bytes=40 * 1024 * 1024
        ),
    )(*[pltpu.with_memory_space_constraint(q, pltpu.HBM) for q in (perm_class, class_values.reshape(1, 8), well_cells.reshape(1, wells), well_rates.reshape(1, wells), guess)])


def solution(mesh):
    whole = P(("real", "space"), None, None, None)
    return jax.shard_map(
        shards,
        mesh=mesh,
        in_specs=(P("space", None, None, None), P(), P("real"), P("real"), whole),
        out_specs=(whole, whole),
        check_vma=False,
    )
```
